256 devices in a mesh: gx: 8 (over x, core), gy: 4 (over z_hi), gz: 8 (over y, z_lo).
Axes of the slice: x: 4, y: 4, z: 8 (z_hi: 4, z_lo: 2; z = z_hi * 2 + z_lo), core: 2. Of those that a mesh axis runs over, the one named last changes fastest.
Arguments:
- tokens: bfloat16 [1536, 5120], P(('gy', 'gx'), 'gz'), may hold values from -8 to 8
- gate_weight: bfloat16 [5120, 13824], P(('gz', 'gy'), 'gx'), may hold values from -0.078125 to 0.078125
- up_weight: bfloat16 [5120, 13824], P(('gz', 'gy'), 'gx'), may hold values from -0.078125 to 0.078125
- down_weight: bfloat16 [13824, 5120], P(('gx', 'gy'), 'gz'), may hold values from -0.0546875 to 0.0546875
- cotangent: bfloat16 [1536, 5120], P(('gy', 'gx'), 'gz'), may hold values from -1.5 to 1.5
- penalty_weight: float32 [5120], P('gz'), may hold values from 0.1 to 1
Outputs:
- mixed: bfloat16 [1536, 5120], P(('gy', 'gx'), 'gz')
- grad_tokens: bfloat16 [1536, 5120], P(('gy', 'gx'), 'gz')
- grad_gate: bfloat16 [5120, 13824], P(('gz', 'gy'), 'gx')
- grad_up: bfloat16 [5120, 13824], P(('gz', 'gy'), 'gx')
- grad_down: bfloat16 [13824, 5120], P(('gx', 'gy'), 'gz')
The draws below stay inside these ranges and needn't reach their ends.
All inputs are finite; a program needn't handle non-finite values.
Results may differ from the reference program's by a relative error of at most 0.01.
Values may be sent and summed in bfloat16 or wider, within the bound.
A program may use at most 128 MiB of HBM per device.

```python
import math
import jax
import jax.numpy as jnp
from jax import lax

D = 5120
F = 13824
TOKENS = 1536


def draw_tokens(key, part):
    key = jax.random.fold_in(key, 11)
    first = jax.random.fold_in(key, 0)
    place = jnp.arange(TOKENS, dtype=jnp.float32) / (TOKENS - 1)
    rising = jnp.exp(0.5 * jnp.log(3.0) * place)[:, None]
    values = jax.random.normal(first, (TOKENS, D), jnp.float32) * rising
    return jnp.clip(values, -8.0, 8.0).astype(jnp.bfloat16)


def block_scale(rng, shape, cuts, least, largest):
    factor_of, own = 1.0, jax.random.fold_in(rng, 6)
    for dim, shards_of in cuts:
        steps = jnp.exp(jax.random.uniform(jax.random.fold_in(own, dim), (shards_of,), jnp.float32, least / len(cuts), largest / len(cuts)))
        factor_of = factor_of * jnp.repeat(steps, shape[dim] // shards_of).reshape([-1 if axis == dim else 1 for axis in range(len(shape))])
    return factor_of


def noise(own_key, shape, scale, reach, pieces=(), kind=jnp.bfloat16):
    array = jax.random.normal(own_key, shape, jnp.float32) * scale
    if len(pieces) > 0:
        array = block_scale(own_key, shape, pieces, -0.22, 0.18) * array
    return jnp.clip(array, min=-reach, max=reach).astype(kind)


def setup_inputs(seed: int = 0) -> dict:
    keys = jax.random.split(jax.random.key(seed), 7)
    return {
        "tokens": draw_tokens(jax.random.fold_in(keys[6], 71), 0),
        "gate_weight": noise(keys[1], (D, F), D ** -0.5, 0.078125, ((0, 32), (1, 8))),
        "up_weight": noise(keys[2], (D, F), D ** -0.5, 0.078125, ((0, 32), (1, 8))),
        "down_weight": noise(keys[3], (F, D), F ** -0.5, 0.0546875, ((0, 32), (1, 8))),
        "cotangent": noise(keys[4], (TOKENS, D), 0.25, 1.5, ((0, 32), (1, 8))),
        "penalty_weight": jnp.clip(jnp.exp(math.log(1.0) - 2.3025851 * jax.random.uniform(keys[5], (D,), jnp.float32) ** block_scale(keys[5], (D,), ((0, 8),), -0.2, 0.2)), 0.1, 1.0),
    }


EPSILON = 1e-05

def moment_sums(values):
    squared = values * values
    return jnp.stack([lax.optimization_barrier(jnp.sum(values, 0)), lax.optimization_barrier(jnp.sum(squared, 0)), lax.optimization_barrier(jnp.sum(squared * values, 0)), lax.optimization_barrier(jnp.sum(squared * squared, 0))])

def penalty_grad(values, totals, count, cotangent, weight):
    mean_value = totals[0] / count
    raw_two = totals[1] / count
    raw_three = totals[2] / count
    raw_four = totals[3] / count
    central_two = raw_two - mean_value * mean_value
    central_three = raw_three - 3.0 * mean_value * raw_two + 2.0 * mean_value * mean_value * mean_value
    central_four = raw_four - 4.0 * mean_value * raw_three + 6.0 * mean_value * mean_value * raw_two - 3.0 * mean_value * mean_value * mean_value * mean_value
    spread = central_two + EPSILON
    centred = values - mean_value
    extra = (centred * centred * centred - central_three) / (spread * spread) - central_four * centred / (spread * spread * spread)
    return (cotangent.astype(jnp.float32) + weight * extra).astype(jnp.bfloat16)

def reference(tokens, gate_weight, up_weight, down_weight, cotangent, penalty_weight):
    gate = jnp.dot(tokens, gate_weight, preferred_element_type=jnp.float32)
    up = jnp.dot(tokens, up_weight, preferred_element_type=jnp.float32)
    sigmoid_gate = jax.nn.sigmoid(gate)
    activated = gate * sigmoid_gate
    hidden = (activated * up).astype(jnp.bfloat16)
    result = jnp.dot(hidden, down_weight, preferred_element_type=jnp.float32)
    mixed = result.astype(jnp.bfloat16)
    totals = moment_sums(result)
    grad_out = penalty_grad(result, totals, float(TOKENS), cotangent, penalty_weight)
    grad_down = jnp.dot(hidden.T, grad_out, preferred_element_type=jnp.float32).astype(jnp.bfloat16)
    grad_hidden = jnp.dot(grad_out, down_weight.T, preferred_element_type=jnp.float32)
    grad_gate_act = (grad_hidden * up * sigmoid_gate * (1.0 + gate * (1.0 - sigmoid_gate))).astype(jnp.bfloat16)
    grad_up_act = (grad_hidden * activated).astype(jnp.bfloat16)
    grad_tokens = (jnp.dot(grad_gate_act, gate_weight.T, preferred_element_type=jnp.float32) + jnp.dot(grad_up_act, up_weight.T, preferred_element_type=jnp.float32)).astype(jnp.bfloat16)
    grad_gate = jnp.dot(tokens.T, grad_gate_act, preferred_element_type=jnp.float32).astype(jnp.bfloat16)
    grad_up = jnp.dot(tokens.T, grad_up_act, preferred_element_type=jnp.float32).astype(jnp.bfloat16)
    return (mixed, grad_tokens, grad_gate, grad_up, grad_down)
```

```python
import jax
import jax.numpy as jnp
from jax import lax
from jax.experimental import pallas as pl
from jax.experimental.pallas import tpu as pltpu
from jax.sharding import PartitionSpec as P

EPSILON = 1e-05
BF, F32 = jnp.bfloat16, jnp.float32
NT = 1536.0
CO = (0, 512, 1024, 1536)
CW = (512, 512, 512, 256)


def dot(a, b):
    return lax.dot_general(a, b, (((1,), (0,)), ((), ())), preferred_element_type=F32)


def dot_t(a, b):
    return lax.dot_general(a, b, (((1,), (1,)), ((), ())), preferred_element_type=F32)


def t_dot(a, b):
    return lax.dot_general(a, b, (((0,), (0,)), ((), ())), preferred_element_type=F32)


def penalty_grad(values, totals, cotangent, weight):
    mean = totals[0:1] / NT
    two = totals[1:2] / NT
    three = totals[2:3] / NT
    four = totals[3:4] / NT
    c2 = two - mean * mean
    c3 = three - 3.0 * mean * two + 2.0 * mean * mean * mean
    c4 = four - 4.0 * mean * three + 6.0 * mean * mean * two - 3.0 * mean * mean * mean * mean
    v = c2 + EPSILON
    d = values - mean
    extra = (d * d * d - c3) / (v * v) - c4 * d / (v * v * v)
    return (cotangent.astype(F32) + weight * extra).astype(BF)


def wide(t, core):
    if t < 3:
        return pl.ds(pl.multiple_of(CO[t] + core * 256, 128), 256)
    return pl.ds(pl.multiple_of(CO[3] + core * 128, 128), 128)


def narrow(t):
    return pl.ds(t * 256, 256 if t < 3 else 128)


def kernel(
    s_ref, tok_ref, wd_ref, cot_ref, pw_ref,
    mixed_ref, dtok_ref, dw_out, gd_ref,
    wf, tokf, pre_s, pre_r, acc, pre2_s, pre2_r, gu,
    h_own, hidf, wdf, y_s, y_r, y2_s, y2_r, mom, mom_r, gyf,
    dh_s, dh_r, dh_p, gd_acc, gd_s, gd_r,
    dgf, dt_acc, dt_s, dt_r, dt2_s, dt2_r, dw_acc, dw_s, dw_r, dw_o,
    s_tz, s_tx, s_wz, s_wl, s_wc, s_py, s_pz, s_h, s_wd, s_wdl, s_yx, s_yz, s_m,
    s_gz, s_gx, s_dh, s_dhp, s_gd, s_gp, s_go, s_gf, s_dtx, s_dtz, s_dwc, s_dwz,
):
    gx, gy, gz = lax.axis_index("gx"), lax.axis_index("gy"), lax.axis_index("gz")
    x, c, zh, y, zl = gx // 2, gx % 2, gy, gz // 2, gz % 2

    def flip(a, k):
        if k == 1:
            return a + 1 - 2 * (a % 2)
        if k == 2:
            return (a + 2) % 4
        if k == 3:
            return 3 - a
        return a

    def dev(dx=0, dc=0, dy=0, dzh=0, dzl=0, zl_at=None):
        zz = zl_at if zl_at is not None else (1 - zl if dzl else zl)
        cc = 1 - c if dc else c
        return (flip(x, dx) * 2 + cc, flip(zh, dzh), flip(y, dy) * 2 + zz)

    pending = []

    def send(src, dst, ss, rs, to):
        cp = pltpu.make_async_remote_copy(
            src_ref=src, dst_ref=dst, send_sem=ss, recv_sem=rs,
            device_id=to, device_id_type=pl.DeviceIdType.MESH,
        )
        cp.start()
        pending.append(cp)
        return cp

    barrier = pltpu.get_barrier_semaphore()
    peers = [dev(dc=1)]
    peers += [dev(dx=d) for d in (1, 2, 3)]
    peers += [dev(dzh=e) for e in (1, 2, 3)]
    peers += [dev(dy=f, dzl=g) for f in range(4) for g in range(2) if (f, g) != (0, 0)]
    for p in peers:
        pl.semaphore_signal(barrier, inc=1, device_id=p, device_id_type=pl.DeviceIdType.MESH)
    pl.semaphore_wait(barrier, len(peers))

    tokf[0, 0] = tok_ref[...]
    tz = [send(tok_ref, tokf.at[e, 0], s_tz.at[0, e - 1], s_tz.at[1, e - 1], dev(dzh=e)) for e in (1, 2, 3)]
    wz, wl = [], []
    for t in range(4):
        cp = pltpu.make_async_copy(s_ref.at[zh, :, narrow(t)], wf.at[zh, :, wide(t, c)], s_wl.at[t])
        cp.start()
        wl.append(cp)
        wz.append([
            send(s_ref.at[flip(zh, e), :, narrow(t)], wf.at[zh, :, wide(t, c)],
                 s_wz.at[0, t, e - 1], s_wz.at[1, t, e - 1], dev(dzh=e))
            for e in (1, 2, 3)
        ])
    wdl, wdr = [], []
    for t in range(4):
        if t < 3:
            src, at = pl.ds(t * 128, 128), pl.ds(pl.multiple_of(t * 256 + c * 128, 16), 128)
        else:
            src, at = pl.ds(384, 48), pl.ds(pl.multiple_of(768 + c * 48, 16), 48)
        cp = pltpu.make_async_copy(wd_ref.at[src], wdf.at[at], s_wdl.at[t])
        cp.start()
        wdl.append(cp)
        wdr.append(send(wd_ref.at[src], wdf.at[at], s_wd.at[0, t], s_wd.at[1, t], dev(dc=1)))
    wdf[864:896, :] = jnp.zeros((32, 640), BF)
    for cp in tz:
        cp.wait_recv()
    tx = [send(tokf.at[:, 0], tokf.at[:, d], s_tx.at[0, d - 1], s_tx.at[1, d - 1], dev(dx=d)) for d in (1, 2, 3)]
    wc = []
    for t in range(4):
        wl[t].wait()
        for cp in wz[t]:
            cp.wait_recv()
        wc.append(send(wf.at[:, :, wide(t, c)], wf.at[:, :, wide(t, c)], s_wc.at[0, t], s_wc.at[1, t], dev(dc=1)))
    for cp in tx:
        cp.wait_recv()

    py, pz = [], []

    def matmul_pre(t):
        wc[t].wait_recv()
        cols = pl.ds(CO[t], CW[t])

        def step(i, _):
            w = wf[:, :, cols].reshape(640, CW[t])
            pre_s[i, :, cols] = dot(tokf[i].reshape(192, 640), w).astype(BF)
            return 0

        lax.fori_loop(0, 4, step, 0)
        py.append([
            send(pre_s.at[flip(y, f), :, cols], pre_r.at[f - 1, :, cols],
                 s_py.at[0, t, f - 1], s_py.at[1, t, f - 1], dev(dy=f))
            for f in (1, 2, 3)
        ])

    def sum_y(t):
        for cp in py[t]:
            cp.wait_recv()
        cols = pl.ds(CO[t], CW[t])

        def half(h):
            rows = pl.ds(pl.multiple_of(h * 96, 16), 96)
            return (
                pre_s[y, rows, cols].astype(F32) + pre_r[0, rows, cols].astype(F32)
            ) + (pre_r[1, rows, cols].astype(F32) + pre_r[2, rows, cols].astype(F32))

        pre2_s[:, cols] = half(1 - zl).astype(BF)
        pz.append(send(pre2_s.at[:, cols], pre2_r.at[:, cols], s_pz.at[0, t], s_pz.at[1, t], dev(dzl=1)))
        acc[:, cols] = half(zl)

    lane = lax.broadcasted_iota(jnp.int32, (96, 128), 1)

    def finish_pre(t):
        pz[t].wait_recv()
        cols = pl.ds(CO[t], CW[t])
        v = acc[:, cols] + pre2_r[:, cols].astype(F32)
        gu[:, cols] = v
        if t < 3:
            for k in range(2):
                g, u = v[:, k * 256 : k * 256 + 128], v[:, k * 256 + 128 : k * 256 + 256]
                h_own[:, t * 256 + k * 128 : t * 256 + k * 128 + 128] = (g * jax.nn.sigmoid(g) * u).astype(BF)
        else:
            hs = []
            for k in range(2):
                g = v[:, k * 128 : k * 128 + 128]
                hs.append(g * jax.nn.sigmoid(g) * pltpu.roll(g, 80, 1))
            tail = jnp.where(lane < 48, hs[0], jnp.where(lane < 96, pltpu.roll(hs[1], 48, 1), 0.0))
            h_own[:, 768:896] = tail.astype(BF)

    for t in range(6):
        if t < 4:
            matmul_pre(t)
        if 0 <= t - 1 < 4:
            sum_y(t - 1)
        if 0 <= t - 2 < 4:
            finish_pre(t - 2)

    hidf[y, zl] = h_own[...]
    hs = {}
    k = 0
    for f, g in ((0, 1), (1, 0), (1, 1), (3, 0), (3, 1), (2, 0), (2, 1)):
        hs[f, g] = send(h_own, hidf.at[y, zl], s_h.at[0, k], s_h.at[1, k], dev(dy=f, dzl=g))
        k += 1
    for cp in wdl:
        cp.wait()
    for cp in wdr:
        cp.wait_recv()

    def reduce_tokens(make_rows, s_buf, r_buf, s2_buf, r2_buf, sem_x, sem_z, order):
        xs = []
        for k, f in enumerate(order):
            e = flip(y, f)
            make_rows(f, e)
            for d in (1, 2, 3):
                xs.append(send(s_buf.at[e, d], r_buf.at[d - 1, e], sem_x.at[0, k, d - 1], sem_x.at[1, k, d - 1], dev(dx=d)))
        for cp in xs:
            cp.wait_recv()
        zs = []

        def total(e):
            return (s_buf[e, 0].astype(F32) + r_buf[0, e].astype(F32)) + (
                r_buf[1, e].astype(F32) + r_buf[2, e].astype(F32)
            )

        for e in (2, 1, 3):
            s2_buf[e - 1] = total(e).astype(BF)
            zs.append(send(s2_buf.at[e - 1], r2_buf.at[e - 1], sem_z.at[0, e - 1], sem_z.at[1, e - 1], dev(dzh=e)))
        own = total(0)
        for cp in zs:
            cp.wait_recv()
        return (own + r2_buf[0].astype(F32)) + (r2_buf[1].astype(F32) + r2_buf[2].astype(F32))

    def y_rows(f, e):
        for g in range(2):
            if (f, g) in hs:
                hs[f, g].wait_recv()
        yb = dot(hidf[e].reshape(192, 896), wdf[...])
        y_s[e] = yb.astype(BF).reshape(4, 48, 640)

    yv = reduce_tokens(y_rows, y_s, y_r, y2_s, y2_r, s_yx, s_yz, (0, 1, 3, 2))
    mixed_ref[...] = yv.astype(BF)

    sq = yv * yv
    mom[0, 0:4] = jnp.concatenate(
        [jnp.sum(v, 0, keepdims=True) for v in (yv, sq, sq * yv, sq * sq)], 0
    )
    mom[0, 4:8] = jnp.zeros((4, 640), F32)
    cp = send(mom.at[0], mom_r.at[0], s_m.at[0, 0], s_m.at[1, 0], dev(dc=1))
    cp.wait_recv()
    mom[1] = mom[0] + mom_r[0]
    cps = [send(mom.at[1], mom_r.at[d], s_m.at[0, d], s_m.at[1, d], dev(dx=d)) for d in (1, 2, 3)]
    for cp in cps:
        cp.wait_recv()
    mom[2] = (mom[1] + mom_r[1]) + (mom_r[2] + mom_r[3])
    cps = [send(mom.at[2], mom_r.at[3 + e], s_m.at[0, 3 + e], s_m.at[1, 3 + e], dev(dzh=e)) for e in (1, 2, 3)]
    for cp in cps:
        cp.wait_recv()
    totals = (mom[2] + mom_r[4]) + (mom_r[5] + mom_r[6])
    gyf[0, 0] = penalty_grad(yv, totals, cot_ref[...], pw_ref[...])

    cps = [send(gyf.at[0, 0], gyf.at[e, 0], s_gz.at[0, e - 1], s_gz.at[1, e - 1], dev(dzh=e)) for e in (1, 2, 3)]
    for cp in cps:
        cp.wait_recv()
    gxs = [send(gyf.at[:, 0], gyf.at[:, d], s_gx.at[0, d - 1], s_gx.at[1, d - 1], dev(dx=d)) for d in (1, 2, 3)]

    def dh_rows(d):
        if d:
            gxs[d - 1].wait_recv()
        v = dot_t(gyf[:, d].reshape(192, 640), wdf[...])
        dh_s[d // 2, :, (d % 2) * 48 : (d % 2) * 48 + 48, :] = v.astype(BF).reshape(4, 48, 896)

    dhs = []
    for p in range(2):
        dh_rows(2 * p)
        dh_rows(2 * p + 1)
        for f in (1, 2, 3):
            dhs.append(send(dh_s.at[p, flip(y, f)], dh_r.at[f - 1, zl],
                            s_dh.at[0, f - 1, p], s_dh.at[1, f - 1, zl], dev(dy=f, zl_at=p)))
    dhp = send(dh_s.at[1 - zl, y], dh_p, s_dhp.at[0], s_dhp.at[1], dev(dzl=1))

    def gd_part(core, t):
        if t < 3:
            h = hidf[:, :, :, pl.ds(pl.multiple_of(t * 256 + core * 128, 128), 128)].reshape(768, 128)
        else:
            h = hidf[:, :, :, 768:896].reshape(768, 128)
        return t_dot(h, gyf[...].reshape(768, 640))

    for t in range(3):
        gd_s[t * 128 : t * 128 + 128] = gd_part(1 - c, t).astype(BF)
    gd_acc[384:512] = gd_part(0, 3)
    gd_s[384:432] = gd_acc[pl.ds(pl.multiple_of(384 + (1 - c) * 48, 8), 48)].astype(BF)
    gdc = send(gd_s, gd_r, s_gd.at[0], s_gd.at[1], dev(dc=1))
    for t in range(3):
        gd_acc[t * 128 : t * 128 + 128] = gd_part(c, t)

    for f in (1, 2, 3):
        for p in range(2):
            pltpu.make_async_remote_copy(
                src_ref=dh_s.at[p, flip(y, f)], dst_ref=dh_r.at[f - 1, p],
                send_sem=s_dh.at[0, f - 1, p], recv_sem=s_dh.at[1, f - 1, p],
                device_id=dev(dy=f, zl_at=p), device_id_type=pl.DeviceIdType.MESH,
            ).wait_recv()
    dhp.wait_recv()

    def dh_at(lo):
        cols = pl.ds(lo, 128)
        v = dh_s[zl, y, :, cols].astype(F32) + dh_p[:, cols].astype(F32)
        for f in range(3):
            v = v + (dh_r[f, 0, :, cols].astype(F32) + dh_r[f, 1, :, cols].astype(F32))
        return v

    def gate_up_grads(dh, g, u):
        sg = jax.nn.sigmoid(g)
        return dh * u * sg * (1.0 + g * (1.0 - sg)), dh * (g * sg)

    gps, gos = [], []
    for t in range(4):
        base = CO[t]
        if t < 3:
            for k in range(2):
                lo = base + k * 256
                dg, du = gate_up_grads(
                    dh_at(t * 256 + k * 128), gu[:, lo : lo + 128], gu[:, lo + 128 : lo + 256]
                )
                dgf[y, zl, :, lo : lo + 128] = dg.astype(BF)
                dgf[y, zl, :, lo + 128 : lo + 256] = du.astype(BF)
        else:
            tail = dh_at(768)
            for k in range(2):
                lo = base + k * 128
                g = gu[:, lo : lo + 128]
                dh = tail if k == 0 else pltpu.roll(tail, 80, 1)
                dg, du = gate_up_grads(dh, g, pltpu.roll(g, 80, 1))
                v = jnp.where(lane < 48, dg, jnp.where(lane < 96, pltpu.roll(du, 48, 1), 0.0))
                dgf[y, zl, :, lo : lo + 128] = v.astype(BF)
        cols = pl.ds(CO[t], CW[t])
        own = dgf.at[y, zl, :, cols]
        gps.append(send(own, own, s_gp.at[0, t], s_gp.at[1, t], dev(dzl=1)))
        gos.append([send(own, own, s_go.at[0, t, f - 1], s_go.at[1, t, f - 1], dev(dy=f)) for f in (1, 2, 3)])

    gfs = []
    for t in range(4):
        cols = pl.ds(CO[t], CW[t])
        gps[t].wait_recv()
        other = dgf.at[y, 1 - zl, :, cols]
        gfs.append([send(other, other, s_gf.at[0, t, f - 1], s_gf.at[1, t, f - 1], dev(dy=f)) for f in (1, 2, 3)])

    gdc.wait_recv()
    gd_ref[0:384] = (gd_acc[0:384] + gd_r[0:384].astype(F32)).astype(BF)
    gd_ref[384:432] = (
        gd_acc[pl.ds(pl.multiple_of(384 + c * 48, 8), 48)] + gd_r[384:432].astype(F32)
    ).astype(BF)

    dwc, dwz = [], []

    def grads_chunk(t):
        for cp in gos[t]:
            cp.wait_recv()
        for cp in gfs[t]:
            cp.wait_recv()
        cols = pl.ds(CO[t], CW[t])
        nc = CW[t] // 2
        for core, buf in ((1 - c, dw_s), (c, dw_acc)):
            v = t_dot(tokf[...].reshape(768, 640), dgf[:, :, :, wide(t, core)].reshape(768, nc))
            buf[:, narrow(t)] = v.astype(buf.dtype)
            if buf is dw_s:
                dwc.append(send(dw_s.at[:, narrow(t)], dw_r.at[:, narrow(t)], s_dwc.at[0, t], s_dwc.at[1, t], dev(dc=1)))

        def step(i, _):
            w = wf[:, :, cols].reshape(640, CW[t])
            v = dot_t(dgf[i, :, :, cols].reshape(192, CW[t]), w)
            dt_acc[i] = v if t == 0 else dt_acc[i] + v
            return 0

        lax.fori_loop(0, 4, step, 0)

    def send_dw(t):
        dwc[t].wait_recv()
        at = narrow(t)
        v = (dw_acc[:, at] + dw_r[:, at].astype(F32)).astype(BF)
        dw_o[:, :, at] = v.reshape(4, 160, v.shape[1])
        cp = pltpu.make_async_copy(dw_o.at[zh, :, at], dw_out.at[zh, :, at], s_wl.at[t])
        cp.start()
        wl2.append(cp)
        dwz.append([
            send(dw_o.at[flip(zh, e), :, at], dw_out.at[zh, :, at],
                 s_dwz.at[0, t, e - 1], s_dwz.at[1, t, e - 1], dev(dzh=e))
            for e in (1, 2, 3)
        ])

    wl2 = []
    for t in range(4):
        grads_chunk(t)
        send_dw(t)

    def dt_rows(f, e):
        dt_s[e] = dt_acc[e].astype(BF).reshape(4, 48, 640)

    dtv = reduce_tokens(dt_rows, dt_s, dt_r, dt2_s, dt2_r, s_dtx, s_dtz, (0, 1, 3, 2))
    dtok_ref[...] = dtv.astype(BF)
    for t in range(4):
        wl2[t].wait()
        for cp in dwz[t]:
            cp.wait_recv()
    for cp in pending:
        cp.wait_send()


def body(tokens, gate_weight, up_weight, down_weight, cotangent, penalty_weight):
    pieces = []
    zero = jnp.zeros((160, 32), BF)
    for j in range(4):
        g = gate_weight[:, 432 * j : 432 * j + 432]
        u = up_weight[:, 432 * j : 432 * j + 432]
        parts = []
        for t in range(3):
            parts += [g[:, 128 * t : 128 * t + 128], u[:, 128 * t : 128 * t + 128]]
        pieces.append(jnp.concatenate(parts + [g[:, 384:], u[:, 384:], zero], 1))
    staged = jnp.stack(pieces)
    V, D = pltpu.VMEM, pltpu.SemaphoreType.DMA
    scratch = [
        V((4, 160, 1792), BF), V((4, 4, 48, 640), BF), V((4, 192, 1792), BF), V((3, 192, 1792), BF),
        V((96, 1792), F32), V((96, 1792), BF), V((96, 1792), BF), V((96, 1792), F32),
        V((96, 896), BF), V((4, 2, 96, 896), BF), V((896, 640), BF),
        V((4, 4, 48, 640), BF), V((3, 4, 48, 640), BF), V((3, 48, 640), BF), V((3, 48, 640), BF),
        V((3, 8, 640), F32), V((7, 8, 640), F32), V((4, 4, 48, 640), BF),
        V((2, 4, 96, 896), BF), V((3, 2, 96, 896), BF), V((96, 896), BF),
        V((512, 640), F32), V((432, 640), BF), V((432, 640), BF),
        V((4, 2, 96, 1792), BF), V((4, 192, 640), F32),
        V((4, 4, 48, 640), BF), V((3, 4, 48, 640), BF), V((3, 48, 640), BF), V((3, 48, 640), BF),
        V((640, 896), F32), V((640, 896), BF), V((640, 896), BF), V((4, 160, 896), BF),
        D((2, 3)), D((2, 3)), D((2, 4, 3)), D((4,)), D((2, 4)), D((2, 4, 3)), D((2, 4)), D((2, 7)),
        D((2, 4)), D((4,)), D((2, 4, 3)), D((2, 3)), D((2, 7)),
        D((2, 3)), D((2, 3)), D((2, 3, 2)), D((2,)), D((2,)), D((2, 4)), D((2, 4, 3)), D((2, 4, 3)),
        D((2, 4, 3)), D((2, 3)), D((2, 4)), D((2, 4, 3)),
    ]
    S = jax.ShapeDtypeStruct
    in_vmem = pl.BlockSpec(memory_space=pltpu.VMEM)
    mixed, grad_tokens, dw, grad_down = pl.pallas_call(
        kernel,
        out_shape=[S((48, 640), BF), S((48, 640), BF), S((4, 160, 896), BF), S((432, 640), BF)],
        in_specs=[in_vmem] * 5,
        out_specs=[in_vmem] * 4,
        scratch_shapes=scratch,
        compiler_params=pltpu.CompilerParams(
            collective_id=0, has_side_effects=True, vmem_limit_bytes=58 * 2**20
        ),
        cost_estimate=pl.CostEstimate(flops=8 * 10**9, bytes_accessed=6 * 10**6, transcendentals=0),
        name="ffn",
    )(staged, tokens, down_weight, cotangent, penalty_weight.reshape(1, 640))

    def assemble(first):
        parts = []
        for j in range(4):
            parts += [dw[j, :, 256 * t + 128 * first : 256 * t + 128 * first + 128] for t in range(3)]
            parts.append(dw[j, :, 768 + 48 * first : 816 + 48 * first])
        return jnp.concatenate(parts, 1)

    return (mixed, grad_tokens, assemble(0), assemble(1), grad_down)


def solution(mesh):
    in_specs = (
        P(("gy", "gx"), "gz"),
        P(("gz", "gy"), "gx"),
        P(("gz", "gy"), "gx"),
        P(("gx", "gy"), "gz"),
        P(("gy", "gx"), "gz"),
        P("gz"),
    )
    out_specs = (
        P(("gy", "gx"), "gz"),
        P(("gy", "gx"), "gz"),
        P(("gz", "gy"), "gx"),
        P(("gz", "gy"), "gx"),
        P(("gx", "gy"), "gz"),
    )
    return jax.shard_map(body, mesh=mesh, in_specs=in_specs, out_specs=out_specs, check_vma=False)
```

```python
import jax
import jax.numpy as jnp
from jax import lax
from jax.experimental import pallas as pl
from jax.experimental.pallas import tpu as pltpu
from jax.sharding import PartitionSpec as P

EPSILON = 1e-05
BF, F32 = jnp.bfloat16, jnp.float32
NT = 1536.0
CO = (0, 512, 1024, 1536)
CW = (512, 512, 512, 256)
SLOTS = 64


def dot(a, b):
    return lax.dot_general(a, b, (((1,), (0,)), ((), ())), preferred_element_type=F32)


def dot_t(a, b):
    return lax.dot_general(a, b, (((1,), (1,)), ((), ())), preferred_element_type=F32)


def t_dot(a, b):
    return lax.dot_general(a, b, (((0,), (0,)), ((), ())), preferred_element_type=F32)


def penalty_grad(values, totals, cotangent, weight):
    mean = totals[0:1] / NT
    two = totals[1:2] / NT
    three = totals[2:3] / NT
    four = totals[3:4] / NT
    c2 = two - mean * mean
    c3 = three - 3.0 * mean * two + 2.0 * mean * mean * mean
    c4 = four - 4.0 * mean * three + 6.0 * mean * mean * two - 3.0 * mean * mean * mean * mean
    v = c2 + EPSILON
    d = values - mean
    extra = (d * d * d - c3) / (v * v) - c4 * d / (v * v * v)
    return (cotangent.astype(F32) + weight * extra).astype(BF)


def cube_root(q):
    r = jnp.exp(jnp.log(jnp.abs(q)) * (1.0 / 3.0))
    return jnp.where(q < 0.0, -r, r)


def wide(t, core):
    if t < 3:
        return pl.ds(pl.multiple_of(CO[t] + core * 256, 128), 256)
    return pl.ds(pl.multiple_of(CO[3] + core * 128, 128), 128)


def narrow(t):
    return pl.ds(t * 256, 256 if t < 3 else 128)


def kernel(
    gw_ref, uw_ref, tok_ref, wd_ref, cot_ref, pw_ref,
    mixed_ref, dtok_ref, dg_ref, du_ref, gd_ref,
    gw, uw, mix, dt_o, gd_o, s_ref, wf, tokf, pre_h, pre_hr, pre_f, pre_s, pre_r, pre_own, acc, pre2_s, pre2_r,
    abf, hidf, wdf, y_own, y_s, y_r, y2_s, y2_r, mom, mom_r, mxf, cotf, gyf,
    dh_s, dh_r, dh_p, gd_acc, gd_s, gd_r, dhf,
    dgf, dt_acc, dt_own, dt_s, dt_r, dt2_s, dt2_r, dw_acc, dw_s, dw_r, dw_o, dw_f,
    s_send, s_in, s_out, s_tz, s_tx, s_wz, s_wl, s_wc, s_ph, s_py, s_pz, s_h, s_wd, s_wdl, s_yx, s_yz, s_m,
    s_gz, s_gx, s_cz, s_cx, s_ab, s_dh, s_dhp, s_gd, s_go, s_g0, s_g1, s_g2, s_dtx, s_dtz, s_dwc, s_dwz,
):
    gx, gy, gz = lax.axis_index("gx"), lax.axis_index("gy"), lax.axis_index("gz")
    x, c, zh, y, zl = gx // 2, gx % 2, gy, gz // 2, gz % 2

    def flip(a, k):
        if k == 1:
            return a + 1 - 2 * (a % 2)
        if k == 2:
            return (a + 2) % 4
        if k == 3:
            return 3 - a
        return a

    def dev(dx=0, dc=0, dy=0, dzh=0, dzl=0, zl_at=None):
        zz = zl_at if zl_at is not None else (1 - zl if dzl else zl)
        cc = 1 - c if dc else c
        return (flip(x, dx) * 2 + cc, flip(zh, dzh), flip(y, dy) * 2 + zz)

    pending, started = {}, [0]

    def send(src, dst, rs, to):
        slot = started[0] % SLOTS
        started[0] += 1
        if slot in pending:
            pending.pop(slot).wait_send()
        cp = pltpu.make_async_remote_copy(
            src_ref=src, dst_ref=dst, send_sem=s_send.at[slot], recv_sem=rs,
            device_id=to, device_id_type=pl.DeviceIdType.MESH,
        )
        cp.start()
        pending[slot] = cp
        return cp

    def sent(cps):
        for slot in [k for k, cp in pending.items() if any(cp is other for other in cps)]:
            pending.pop(slot).wait_send()

    barrier = pltpu.get_barrier_semaphore()
    peers = [dev(dx=d, dc=k) for d in range(4) for k in range(2) if (d, k) != (0, 0)]
    peers += [dev(dzh=e) for e in (1, 2, 3)]
    peers += [dev(dy=f, dzl=g) for f in range(4) for g in range(2) if (f, g) != (0, 0)]
    for p in peers:
        pl.semaphore_signal(barrier, inc=1, device_id=p, device_id_type=pl.DeviceIdType.MESH)
    ins = [
        pltpu.make_async_copy(src, to, s_in.at[k])
        for k, (src, to) in enumerate(((tok_ref, tokf.at[0, 0]), (gw_ref, gw), (uw_ref, uw), (cot_ref, cotf.at[0, 0])))
    ]
    for cp in ins:
        cp.start()
    lane160 = lax.broadcasted_iota(jnp.int32, (160, 128), 1)

    def shifted(ref, lo, at):
        base = lo // 128 * 128
        v = ref[:, base : min(base + 256, 1728)].astype(F32)
        if v.shape[1] < 256:
            v = jnp.concatenate([v, jnp.zeros((160, 256 - v.shape[1]), F32)], 1)
        r = (at - (lo - base)) % 256
        return (pltpu.roll(v, r, 1) if r else v)[:, 0:128]

    def stage(t):
        for j in range(4):
            if t < 3:
                for k, ref in enumerate((gw, uw)):
                    s_ref[j, :, t * 256 + k * 128 : t * 256 + k * 128 + 128] = shifted(ref, 432 * j + 128 * t, 0).astype(BF)
            else:
                g, u = shifted(gw, 432 * j + 384, 0), shifted(uw, 432 * j + 384, 48)
                s_ref[j, :, 768:896] = jnp.where(lane160 < 48, g, jnp.where(lane160 < 96, u, 0.0)).astype(BF)

    for cp in ins:
        cp.wait()
    stage(0)
    pl.semaphore_wait(barrier, len(peers))

    tz = [send(tokf.at[0, 0], tokf.at[e, 0], s_tz.at[e - 1], dev(dzh=e)) for e in (1, 3, 2)]
    wz, wl, wc = [], [], []

    def issue_w(t):
        cp = pltpu.make_async_copy(s_ref.at[zh, :, narrow(t)], wf.at[zh, :, wide(t, c)], s_wl.at[t])
        cp.start()
        wl.append(cp)
        wz.append([
            send(s_ref.at[flip(zh, e), :, narrow(t)], wf.at[zh, :, wide(t, c)],
                 s_wz.at[t, e - 1], dev(dzh=e))
            for e in (2, 1, 3)
        ])

    def forward_w(t):
        wl[t].wait()
        for cp in wz[t]:
            cp.wait_recv()
        wc.append(send(wf.at[:, :, wide(t, c)], wf.at[:, :, wide(t, c)], s_wc.at[t], dev(dc=1)))

    tx = [send(tokf.at[0, 0], tokf.at[0, d], s_tx.at[d - 1], dev(dx=d)) for d in (2, 1, 3)]
    stage(1)
    sent(tz)
    issue_w(0)
    stage(2)
    for e, cp in zip((1, 3, 2), tz):
        cp.wait_recv()
        tx += [send(tokf.at[e, 0], tokf.at[e, d], s_tx.at[3 * e + d - 1], dev(dx=d)) for d in (2, 1, 3)]
    stage(3)
    wdl, wdr = [], []
    for t in range(4):
        if t < 3:
            src, at = pl.ds(t * 128, 128), pl.ds(pl.multiple_of(t * 256 + c * 128, 16), 128)
        else:
            src, at = pl.ds(384, 48), pl.ds(pl.multiple_of(768 + c * 48, 16), 48)
        cp = pltpu.make_async_copy(wd_ref.at[src], wdf.at[at], s_wdl.at[t])
        cp.start()
        wdl.append(cp)
        wdr.append(send(wd_ref.at[src], wdf.at[at], s_wd.at[t], dev(dc=1)))
    wdf[864:896, :] = jnp.zeros((32, 640), BF)

    py, pz = [], []

    halves = []

    def matmul_pre(t):
        wc[t].wait_recv()
        cols = pl.ds(CO[t], CW[t])
        for f in (2, 1, 3, 0):
            w = wf[:, :, cols].reshape(640, CW[t])
            v = dot(tokf[flip(y, f)].reshape(192, 640), w)
            if f == 2:
                pre_h[:, cols] = v.astype(BF)
                halves.append([
                    send(pre_h.at[96 * k : 96 * k + 96, cols], pre_hr.at[k, :, cols], s_ph.at[t, k],
                         dev(dy=1 + 2 * k))
                    for k in range(2)
                ])
            elif f:
                pre_f[f // 2, :, cols] = v
            else:
                pre_own[:, cols] = v

    def relay(t):
        for cp in halves[t]:
            cp.wait_recv()
        cols = pl.ds(CO[t], CW[t])
        pre_s[0, 0:96, cols] = pre_f[0, 0:96, cols].astype(BF)
        pre_s[0, 96:192, cols] = (pre_f[0, 96:192, cols] + pre_hr[1, :, cols].astype(F32)).astype(BF)
        pre_s[1, 0:96, cols] = (pre_f[1, 0:96, cols] + pre_hr[0, :, cols].astype(F32)).astype(BF)
        pre_s[1, 96:192, cols] = pre_f[1, 96:192, cols].astype(BF)
        py.append([
            send(pre_s.at[k, :, cols], pre_r.at[k, :, cols], s_py.at[t, k], dev(dy=1 + 2 * k))
            for k in range(2)
        ])

    def sum_y(t):
        for cp in py[t]:
            cp.wait_recv()
        cols = pl.ds(CO[t], CW[t])

        def half(h):
            rows = pl.ds(pl.multiple_of(h * 96, 16), 96)
            return pre_own[rows, cols] + (pre_r[0, rows, cols].astype(F32) + pre_r[1, rows, cols].astype(F32))

        other = half(1 - zl)
        pre2_s[:, cols] = (other * other * other).astype(BF)
        pz.append(send(pre2_s.at[:, cols], pre2_r.at[:, cols], s_pz.at[t], dev(dzl=1)))
        acc[:, cols] = half(zl)

    lane = lax.broadcasted_iota(jnp.int32, (96, 128), 1)

    def factors(g, u):
        sg = jax.nn.sigmoid(g)
        act = g * sg
        return act * u, u * sg * (1.0 + g * (1.0 - sg)), act

    def finish_pre(t):
        pz[t].wait_recv()
        cols = pl.ds(CO[t], CW[t])
        v = acc[:, cols] + cube_root(pre2_r[:, cols].astype(F32))
        if t < 3:
            for k in range(2):
                h, fa, fb = factors(v[:, k * 256 : k * 256 + 128], v[:, k * 256 + 128 : k * 256 + 256])
                lo = CO[t] + k * 256
                hidf[y, zl, :, t * 256 + k * 128 : t * 256 + k * 128 + 128] = h.astype(BF)
                abf[y, zl, :, lo : lo + 128] = fa.astype(BF)
                abf[y, zl, :, lo + 128 : lo + 256] = fb.astype(BF)
        else:
            hs = []
            for k in range(2):
                g = v[:, k * 128 : k * 128 + 128]
                h, fa, fb = factors(g, pltpu.roll(g, 80, 1))
                hs.append(h)
                lo = CO[3] + k * 128
                abf[y, zl, :, lo : lo + 128] = jnp.where(
                    lane < 48, fa, jnp.where(lane < 96, pltpu.roll(fb, 48, 1), 0.0)
                ).astype(BF)
            tail = jnp.where(lane < 48, hs[0], jnp.where(lane < 96, pltpu.roll(hs[1], 48, 1), 0.0))
            hidf[y, zl, :, 768:896] = tail.astype(BF)

    sent(wz[0])
    issue_w(1)
    forward_w(0)
    for cp in tx:
        cp.wait_recv()
    matmul_pre(0)
    sent(wz[1])
    issue_w(2)
    forward_w(1)
    matmul_pre(1)
    relay(0)
    sent(wz[2])
    issue_w(3)
    forward_w(2)
    cz = [send(cotf.at[0, 0], cotf.at[e, 0], s_cz.at[e - 1], dev(dzh=e)) for e in (2, 1, 3)]
    matmul_pre(2)
    relay(1)
    sum_y(0)
    forward_w(3)
    relay(2)
    matmul_pre(3)
    sum_y(1)
    relay(3)
    finish_pre(0)
    sum_y(2)
    for cp in cz:
        cp.wait_recv()
    cxs = [send(cotf.at[:, 0], cotf.at[:, d], s_cx.at[d - 1], dev(dx=d)) for d in (2, 1, 3)]
    sum_y(3)
    finish_pre(1)
    finish_pre(2)
    finish_pre(3)

    class Gather:
        def __init__(self, ref, sems, cols):
            self.ref, self.sems, self.cols, self.cps = ref, sems, cols, {}

        def go(self, k, a, b, to, rows=pl.ds(0, 96)):
            block = self.ref.at[a, b, rows, self.cols]
            self.cps[k] = send(block, block, self.sems.at[k], to)

        def start_z(self):
            self.go(0, y, zl, dev(dzl=1))

        def start(self):
            for k in range(2):
                self.go(1 + k, y, zl, dev(dy=1 + 2 * k))

        def neighbour(self):
            self.cps[0].wait_recv()
            for k in range(2):
                self.go(3 + k, y, 1 - zl, dev(dy=1 + 2 * k))

        def onward(self, g):
            for k in range(2):
                self.cps[1 + 2 * g + k].wait_recv()
                z = 1 - zl if g else zl
                self.go(5 + 2 * g + k, flip(y, 1 + 2 * k), z, dev(dy=3 - 2 * k), pl.ds(48 * k, 48))

        def finish(self):
            for k in range(5, 9):
                self.cps[k].wait_recv()

    hid = Gather(hidf, s_h, pl.ds(0, 896))
    hid.start_z()
    hid.start()
    for cp in wdl:
        cp.wait()
    for cp in wdr:
        cp.wait_recv()
    hid.neighbour()
    ab = Gather(abf, s_ab, pl.ds(0, 1792))
    ab.start_z()

    def reduce_tokens(make_rows, own_buf, s_buf, r_buf, s2_buf, r2_buf, sem_x, sem_z, order, between=None):
        xs = []
        for k, f in enumerate(order):
            e = flip(y, f)
            v = make_rows(f, e).reshape(4, 48, 640)
            own_buf[e] = v[0]
            s_buf[e] = v[1:4].astype(BF)
            for d in (2, 1, 3):
                xs.append(send(s_buf.at[e, d - 1], r_buf.at[d - 1, e], sem_x.at[k, d - 1], dev(dx=d)))
        if between is not None:
            between()
        for cp in xs:
            cp.wait_recv()
        zs = []

        def total(e):
            return (own_buf[e] + r_buf[0, e].astype(F32)) + (
                r_buf[1, e].astype(F32) + r_buf[2, e].astype(F32)
            )

        for e in (2, 1, 3):
            s2_buf[e - 1] = total(e).astype(BF)
            zs.append(send(s2_buf.at[e - 1], r2_buf.at[e - 1], sem_z.at[e - 1], dev(dzh=e)))
        own = total(0)
        for cp in zs:
            cp.wait_recv()
        return (own + r2_buf[0].astype(F32)) + (r2_buf[1].astype(F32) + r2_buf[2].astype(F32))

    def y_rows(f, e):
        if f == 1:
            hid.onward(0)
            hid.onward(1)
        elif f == 2:
            hid.finish()
        return dot(hidf[e].reshape(192, 896), wdf[...])

    def after_y():
        ab.start()
        ab.neighbour()

    yv = reduce_tokens(y_rows, y_own, y_s, y_r, y2_s, y2_r, s_yx, s_yz, (0, 1, 3, 2), after_y)

    sq = yv * yv
    mom[0, 0:4] = jnp.concatenate(
        [jnp.sum(v, 0, keepdims=True) for v in (yv, sq, sq * yv, sq * sq)], 0
    )
    mom[0, 4:8] = jnp.zeros((4, 640), F32)
    cps = [
        send(mom.at[0], mom_r.at[2 * d + k - 1], s_m.at[2 * d + k - 1], dev(dx=d, dc=k))
        for d in (2, 1, 3, 0) for k in (1, 0) if (d, k) != (0, 0)
    ]
    mxf[0, 0] = (sq * yv).astype(BF)
    mz = [send(mxf.at[0, 0], mxf.at[e, 0], s_gz.at[e - 1], dev(dzh=e)) for e in (1, 3, 2)]
    mx = {d: [send(mxf.at[0, 0], mxf.at[0, d], s_gx.at[d - 1], dev(dx=d))] for d in (2, 1, 3)}
    mix[...] = yv.astype(BF)
    outs = [pltpu.make_async_copy(mix, mixed_ref, s_out.at[0])]
    outs[0].start()
    for cp in cps:
        cp.wait_recv()
    mom[1] = ((mom[0] + mom_r[0]) + (mom_r[1] + mom_r[2])) + ((mom_r[3] + mom_r[4]) + (mom_r[5] + mom_r[6]))
    ms = [send(mom.at[1], mom_r.at[6 + e], s_m.at[6 + e], dev(dzh=e)) for e in (2, 1, 3)]
    for e, cp in zip((1, 3, 2), mz):
        cp.wait_recv()
        for d in (2, 1, 3):
            mx[d].append(send(mxf.at[e, 0], mxf.at[e, d], s_gx.at[3 * e + d - 1], dev(dx=d)))
    ab.onward(0)
    ab.onward(1)
    for cp in ms:
        cp.wait_recv()
    mom[2] = (mom[1] + mom_r[7]) + (mom_r[8] + mom_r[9])
    for cp in cxs:
        cp.wait_recv()

    def dh_rows(d):
        if d:
            for cp in mx[d]:
                cp.wait_recv()
        totals, weight = mom[2], pw_ref[...].reshape(1, 640)
        for e in range(4):
            gyf[e, d] = penalty_grad(cube_root(mxf[e, d].astype(F32)), totals, cotf[e, d], weight)
        v = dot_t(gyf[:, d].reshape(192, 640), wdf[...])
        dh_s[d // 2, :, (d % 2) * 48 : (d % 2) * 48 + 48, :] = v.astype(BF).reshape(4, 48, 896)

    for d in (0, 1, 3, 2):
        dh_rows(d)
        p, q = d // 2, d % 2
        rows = pl.ds(48 * q, 48)
        for f in (2, 1, 3):
            send(dh_s.at[p, flip(y, f), rows], dh_r.at[f - 1, zl, rows],
                 s_dh.at[f - 1, zl, q], dev(dy=f, zl_at=p))
    dhp = send(dh_s.at[1 - zl, y], dh_p, s_dhp.at[0], dev(dzl=1))

    def gd_part(core, t):
        if t < 3:
            h = hidf[:, :, :, pl.ds(pl.multiple_of(t * 256 + core * 128, 128), 128)].reshape(768, 128)
        else:
            h = hidf[:, :, :, 768:896].reshape(768, 128)
        return t_dot(h, gyf[...].reshape(768, 640))

    for t in range(3):
        gd_s[t * 128 : t * 128 + 128] = gd_part(1 - c, t).astype(BF)
    gd_acc[384:512] = gd_part(0, 3)
    gd_s[384:432] = gd_acc[pl.ds(pl.multiple_of(384 + (1 - c) * 48, 8), 48)].astype(BF)
    gdc = send(gd_s, gd_r, s_gd.at[0], dev(dc=1))
    for t in range(3):
        gd_acc[t * 128 : t * 128 + 128] = gd_part(c, t)

    for f in (1, 2, 3):
        for p in range(2):
            for q in range(2):
                rows = pl.ds(48 * q, 48)
                pltpu.make_async_remote_copy(
                    src_ref=dh_s.at[p, flip(y, f), rows], dst_ref=dh_r.at[f - 1, p, rows],
                    send_sem=s_send.at[0], recv_sem=s_dh.at[f - 1, p, q],
                    device_id=dev(dy=f, zl_at=p), device_id_type=pl.DeviceIdType.MESH,
                ).wait_recv()
    dhp.wait_recv()

    HO, HW = (0, 256, 512, 768), (256, 256, 256, 128)
    def sum_dh(t):
        cols = pl.ds(HO[t], HW[t])
        v = dh_s[zl, y, :, cols].astype(F32) + dh_p[:, cols].astype(F32)
        for f in range(3):
            v = v + (dh_r[f, 0, :, cols].astype(F32) + dh_r[f, 1, :, cols].astype(F32))
        dhf[y, zl, :, cols] = v.astype(BF)

    sum_dh(3)
    own = dhf.at[y, zl, :, pl.ds(HO[3], HW[3])]
    first = [
        send(own, own, s_go.at[2 * f + g - 1], dev(dy=f, dzl=g))
        for f, g in ((2, 1), (2, 0), (1, 1), (3, 1), (1, 0), (3, 0), (0, 1))
    ]
    for t in range(3):
        sum_dh(t)
    dhg = [Gather(dhf, sems, pl.ds(HO[t], HW[t])) for t, sems in enumerate((s_g0, s_g1, s_g2))]

    gdc.wait_recv()
    gd_o[0:384] = (gd_acc[0:384] + gd_r[0:384].astype(F32)).astype(BF)
    gd_o[384:432] = (
        gd_acc[pl.ds(pl.multiple_of(384 + c * 48, 8), 48)] + gd_r[384:432].astype(F32)
    ).astype(BF)
    ab.finish()
    outs.append(pltpu.make_async_copy(gd_o, gd_ref, s_out.at[1]))
    outs[1].start()

    dwc, dwz, dwl = {}, {}, {}

    def grads_chunk(t):
        if t < 3:
            dhg[t].finish()
        else:
            for cp in first:
                cp.wait_recv()
        cols = pl.ds(CO[t], CW[t])

        def multiply(i, _):
            e, g = i // 2, i % 2
            if t < 3:
                for k in range(2):
                    dh = dhf[e, g, :, t * 256 + k * 128 : t * 256 + k * 128 + 128].astype(F32)
                    for m in range(2):
                        at = pl.ds(CO[t] + k * 256 + m * 128, 128)
                        dgf[e, g, :, at] = (dh * abf[e, g, :, at].astype(F32)).astype(BF)
            else:
                dh = dhf[e, g, :, 768:896].astype(F32)
                for k in range(2):
                    one = jnp.where(lane < 48, dh if k == 0 else pltpu.roll(dh, 80, 1), 0.0)
                    at = pl.ds(CO[3] + k * 128, 128)
                    both = one + pltpu.roll(one, 48, 1)
                    dgf[e, g, :, at] = (both * abf[e, g, :, at].astype(F32)).astype(BF)
            return 0

        lax.fori_loop(0, 8, multiply, 0)

    def dw_chunk(t):
        nc = CW[t] // 2
        for core, buf in ((1 - c, dw_s), (c, dw_acc)):
            v = t_dot(tokf[...].reshape(768, 640), dgf[:, :, :, wide(t, core)].reshape(768, nc))
            buf[:, narrow(t)] = v.astype(buf.dtype)
            if buf is dw_s:
                dwc[t] = send(dw_s.at[:, narrow(t)], dw_r.at[:, narrow(t)], s_dwc.at[t], dev(dc=1))

    def dt_chunk(t):
        cols = pl.ds(CO[t], CW[t])
        for i in range(2):
            w = wf[:, :, cols].reshape(640, CW[t])
            v = dot_t(dgf[2 * i : 2 * i + 2, :, :, cols].reshape(384, CW[t]), w).reshape(2, 192, 640)
            dt_acc[2 * i : 2 * i + 2] = v if t == 3 else dt_acc[2 * i : 2 * i + 2] + v

    def send_dw(t):
        dwc[t].wait_recv()
        at = narrow(t)
        v = (dw_acc[:, at] + dw_r[:, at].astype(F32)).astype(BF)
        dw_o[:, :, at] = v.reshape(4, 160, v.shape[1])
        cp = pltpu.make_async_copy(dw_o.at[zh, :, at], dw_f.at[zh, :, at], s_wl.at[t])
        cp.start()
        dwl[t] = cp
        dwz[t] = [
            send(dw_o.at[flip(zh, e), :, at], dw_f.at[zh, :, at],
                 s_dwz.at[t, e - 1], dev(dzh=e))
            for e in (2, 1, 3)
        ]

    sent(first)
    dhg[0].start_z()
    dhg[0].start()
    grads_chunk(3)
    dw_chunk(3)
    dhg[0].neighbour()
    dhg[1].start_z()
    dhg[1].start()
    dt_chunk(3)
    send_dw(3)
    dhg[0].onward(0)
    dhg[0].onward(1)
    dhg[1].neighbour()
    dhg[2].start_z()
    dhg[2].start()
    grads_chunk(0)
    dw_chunk(0)
    dt_chunk(0)
    dhg[1].onward(0)
    send_dw(0)
    dhg[1].onward(1)
    dhg[2].neighbour()
    grads_chunk(1)
    dw_chunk(1)
    dt_chunk(1)
    dhg[2].onward(0)
    send_dw(1)
    dhg[2].onward(1)
    grads_chunk(2)
    dt_chunk(2)

    def last_dw():
        dw_chunk(2)
        send_dw(2)

    dtv = reduce_tokens(lambda f, e: dt_acc[e], dt_own, dt_s, dt_r, dt2_s, dt2_r, s_dtx, s_dtz, (0, 1, 3, 2), last_dw)
    dt_o[...] = dtv.astype(BF)
    outs.append(pltpu.make_async_copy(dt_o, dtok_ref, s_out.at[2]))
    outs[2].start()
    for t in range(4):
        dwl[t].wait()
        for cp in dwz[t]:
            cp.wait_recv()
    for m, out, to in ((0, gw, dg_ref), (1, uw, du_ref)):
        for n in range(14):
            total = None
            for j in range(4):
                for t in range(4):
                    lo = 432 * j + 128 * t
                    size = 128 if t < 3 else 48
                    if lo + size <= 128 * n or lo >= 128 * n + 128:
                        continue
                    at, off = (t * 256 + m * 128, 0) if t < 3 else (768, 48 * m)
                    v = dw_f[j, :, at : at + 128].astype(F32)
                    r = (lo - 128 * n - off) % 128
                    v = pltpu.roll(v, r, 1) if r else v
                    first, last = max(lo - 128 * n, 0), min(lo + size - 128 * n, 128)
                    keep = (lane160 >= first) & (lane160 < last)
                    total = jnp.where(keep, v, 0.0 if total is None else total)
            total = total.astype(BF)
            if n < 13:
                out[:, 128 * n : 128 * n + 128] = total
            else:
                out[:, 1664:1728] = total[:, 0:64]
        outs.append(pltpu.make_async_copy(out, to, s_out.at[3 + m]))
        outs[3 + m].start()
    for cp in outs:
        cp.wait()
    for cp in pending.values():
        cp.wait_send()


def hand_over(*refs):
    for k in range(5):
        refs[5 + k][...] = refs[k][...]


def body(tokens, gate_weight, up_weight, down_weight, cotangent, penalty_weight):
    V, D = pltpu.VMEM, pltpu.SemaphoreType.DMA
    scratch = [
        V((160, 1728), BF), V((160, 1728), BF), V((48, 640), BF), V((48, 640), BF), V((432, 640), BF), V((4, 160, 896), BF),
        V((4, 160, 1792), BF), V((4, 4, 48, 640), BF), V((192, 1792), BF), V((2, 96, 1792), BF), V((2, 192, 1792), F32),
        V((2, 192, 1792), BF), V((2, 192, 1792), BF),
        V((192, 1792), F32), V((96, 1792), F32), V((96, 1792), BF), V((96, 1792), BF),
        V((4, 2, 96, 1792), BF), V((4, 2, 96, 896), BF), V((896, 640), BF),
        V((4, 48, 640), F32), V((4, 3, 48, 640), BF), V((3, 4, 48, 640), BF), V((3, 48, 640), BF), V((3, 48, 640), BF),
        V((3, 8, 640), F32), V((10, 8, 640), F32), V((4, 4, 48, 640), BF), V((4, 4, 48, 640), BF), V((4, 4, 48, 640), BF),
        V((2, 4, 96, 896), BF), V((3, 2, 96, 896), BF), V((96, 896), BF),
        V((512, 640), F32), V((432, 640), BF), V((432, 640), BF), V((4, 2, 96, 896), BF),
        V((4, 2, 96, 1792), BF), V((4, 192, 640), F32),
        V((4, 48, 640), F32), V((4, 3, 48, 640), BF), V((3, 4, 48, 640), BF), V((3, 48, 640), BF), V((3, 48, 640), BF),
        V((640, 896), F32), V((640, 896), BF), V((640, 896), BF), V((4, 160, 896), BF), V((4, 160, 896), BF),
        D((SLOTS,)), D((4,)), D((5,)), D((3,)), D((12,)), D((4, 3)), D((4,)), D((4,)), D((4, 2)), D((4, 2)), D((4,)), D((9,)),
        D((4,)), D((4,)), D((4, 3)), D((3,)), D((10,)),
        D((3,)), D((12,)), D((3,)), D((3,)), D((9,)),
        D((3, 2, 2)), D((1,)), D((1,)), D((7,)), D((9,)), D((9,)), D((9,)),
        D((4, 3)), D((3,)), D((4,)), D((4, 3)),
    ]
    S = jax.ShapeDtypeStruct
    in_vmem = pl.BlockSpec(memory_space=pltpu.VMEM)
    in_any = pl.BlockSpec(memory_space=pl.ANY)
    shapes = [S((48, 640), BF), S((48, 640), BF), S((160, 1728), BF), S((160, 1728), BF), S((432, 640), BF)]
    results = pl.pallas_call(
        kernel,
        out_shape=shapes,
        in_specs=[in_any] * 5 + [in_vmem],
        out_specs=[in_any] * 5,
        scratch_shapes=scratch,
        compiler_params=pltpu.CompilerParams(
            collective_id=0, has_side_effects=True, vmem_limit_bytes=58 * 2**20
        ),
        cost_estimate=pl.CostEstimate(flops=8 * 10**9, bytes_accessed=6 * 10**6, transcendentals=0),
        name="ffn",
    )(gate_weight, up_weight, tokens, down_weight, cotangent, penalty_weight)
    return tuple(
        pl.pallas_call(
            hand_over,
            out_shape=shapes,
            in_specs=[in_vmem] * 5,
            out_specs=[in_vmem] * 5,
            name="hand_over",
        )(*results)
    )


def solution(mesh):
    in_specs = (
        P(("gy", "gx"), "gz"),
        P(("gz", "gy"), "gx"),
        P(("gz", "gy"), "gx"),
        P(("gx", "gy"), "gz"),
        P(("gy", "gx"), "gz"),
        P("gz"),
    )
    out_specs = (
        P(("gy", "gx"), "gz"),
        P(("gy", "gx"), "gz"),
        P(("gz", "gy"), "gx"),
        P(("gz", "gy"), "gx"),
        P(("gx", "gy"), "gz"),
    )
    return jax.shard_map(body, mesh=mesh, in_specs=in_specs, out_specs=out_specs, check_vma=False)
```

```python
import jax
import jax.numpy as jnp
from jax import lax
from jax.experimental import pallas as pl
from jax.experimental.pallas import tpu as pltpu
from jax.sharding import PartitionSpec as P

EPSILON = 1e-05
BF, F32 = jnp.bfloat16, jnp.float32
NT = 1536.0
CO = (0, 512, 1024, 1536)
CW = (512, 512, 512, 256)
SLOTS = 48


def dot(a, b):
    return lax.dot_general(a, b, (((1,), (0,)), ((), ())), preferred_element_type=F32)


def dot_t(a, b):
    return lax.dot_general(a, b, (((1,), (1,)), ((), ())), preferred_element_type=F32)


def t_dot(a, b):
    return lax.dot_general(a, b, (((0,), (0,)), ((), ())), preferred_element_type=F32)


def penalty_grad(values, totals, cotangent, weight):
    mean = totals[0:1] / NT
    two = totals[1:2] / NT
    three = totals[2:3] / NT
    four = totals[3:4] / NT
    c2 = two - mean * mean
    c3 = three - 3.0 * mean * two + 2.0 * mean * mean * mean
    c4 = four - 4.0 * mean * three + 6.0 * mean * mean * two - 3.0 * mean * mean * mean * mean
    v = c2 + EPSILON
    d = values - mean
    extra = (d * d * d - c3) / (v * v) - c4 * d / (v * v * v)
    return (cotangent.astype(F32) + weight * extra).astype(BF)


def cube_root(q):
    r = jnp.exp(jnp.log(jnp.abs(q)) * (1.0 / 3.0))
    return jnp.where(q < 0.0, -r, r)


def wide(t, core):
    if t < 3:
        return pl.ds(pl.multiple_of(CO[t] + core * 256, 128), 256)
    return pl.ds(pl.multiple_of(CO[3] + core * 128, 128), 128)


def narrow(t):
    return pl.ds(t * 256, 256 if t < 3 else 128)


def kernel(
    gw_ref, uw_ref, tok_ref, wd_ref, cot_ref, pw_ref,
    mixed_ref, dtok_ref, dg_ref, du_ref, gd_ref,
    gw, uw, mix, dt_o, gd_o, s_ref, wf, tokf, pre_h, pre_hr, pre_f, pre_s, pre_r, pre_own, acc, pre2_s, pre2_r,
    abf, hidf, wdf, y_own, y_s, y_r, y2_s, y2_r, mom, mom_r, mxf, cotf, gyf,
    dh_s, dh_r, dh_p, gd_acc, gd_s, gd_r, dhf,
    dgf, dt_acc, dt_own, dt_s, dt_r, dt2_s, dt2_r, dw_acc, dw_s, dw_r, dw_o, dw_f,
    s_send, s_in, s_out, s_tz, s_tx, s_wz, s_wl, s_wc, s_ph, s_py, s_pz, s_h, s_h2, s_wd, s_wdl, s_yx, s_yz, s_ys, s_m,
    s_gz, s_gx, s_cz, s_cx, s_ab, s_dh, s_dhp, s_gd, s_go, s_g0, s_g1, s_g2, s_dtx, s_dtz, s_dwc, s_dwz,
):
    gx, gy, gz = lax.axis_index("gx"), lax.axis_index("gy"), lax.axis_index("gz")
    x, c, zh, y, zl = gx // 2, gx % 2, gy, gz // 2, gz % 2

    def flip(a, k):
        if k == 1:
            return a + 1 - 2 * (a % 2)
        if k == 2:
            return (a + 2) % 4
        if k == 3:
            return 3 - a
        return a

    def dev(dx=0, dc=0, dy=0, dzh=0, dzl=0, zl_at=None):
        zz = zl_at if zl_at is not None else (1 - zl if dzl else zl)
        cc = 1 - c if dc else c
        return (flip(x, dx) * 2 + cc, flip(zh, dzh), flip(y, dy) * 2 + zz)

    pending, started = {}, [0]

    def send(src, dst, rs, to):
        slot = started[0] % SLOTS
        started[0] += 1
        if slot in pending:
            pending.pop(slot).wait_send()
        cp = pltpu.make_async_remote_copy(
            src_ref=src, dst_ref=dst, send_sem=s_send.at[slot], recv_sem=rs,
            device_id=to, device_id_type=pl.DeviceIdType.MESH,
        )
        cp.start()
        pending[slot] = cp
        return cp

    def arrive(ref, sem):
        pltpu.make_async_remote_copy(
            src_ref=ref, dst_ref=ref, send_sem=s_send.at[0], recv_sem=sem,
            device_id=dev(dc=1), device_id_type=pl.DeviceIdType.MESH,
        ).wait_recv()

    def sent(cps):
        for slot in [k for k, cp in pending.items() if any(cp is other for other in cps)]:
            pending.pop(slot).wait_send()

    barrier = pltpu.get_barrier_semaphore()
    peers = [dev(dx=d, dc=k) for d in range(4) for k in range(2) if (d, k) != (0, 0)]
    peers += [dev(dzh=e) for e in (1, 2, 3)]
    peers += [dev(dy=f, dzl=g) for f in range(4) for g in range(2) if (f, g) != (0, 0)]
    for p in peers:
        pl.semaphore_signal(barrier, inc=1, device_id=p, device_id_type=pl.DeviceIdType.MESH)
    ins = [
        pltpu.make_async_copy(src, to, s_in.at[k])
        for k, (src, to) in enumerate(((tok_ref, tokf.at[0, 0]), (gw_ref, gw), (uw_ref, uw), (cot_ref, cotf.at[0, 0])))
    ]
    for cp in ins:
        cp.start()
    lane160 = lax.broadcasted_iota(jnp.int32, (160, 128), 1)

    def shifted(ref, lo, at):
        base = lo // 128 * 128
        v = ref[:, base : min(base + 256, 1728)].astype(F32)
        if v.shape[1] < 256:
            v = jnp.concatenate([v, jnp.zeros((160, 256 - v.shape[1]), F32)], 1)
        r = (at - (lo - base)) % 256
        return (pltpu.roll(v, r, 1) if r else v)[:, 0:128]

    def stage(t):
        for j in range(4):
            if t < 3:
                for k, ref in enumerate((gw, uw)):
                    s_ref[j, :, t * 256 + k * 128 : t * 256 + k * 128 + 128] = shifted(ref, 432 * j + 128 * t, 0).astype(BF)
            else:
                g, u = shifted(gw, 432 * j + 384, 0), shifted(uw, 432 * j + 384, 48)
                s_ref[j, :, 768:896] = jnp.where(lane160 < 48, g, jnp.where(lane160 < 96, u, 0.0)).astype(BF)

    for cp in ins:
        cp.wait()
    stage(0)
    pl.semaphore_wait(barrier, len(peers))

    class Gather:
        def __init__(self, ref, sems, cols):
            self.ref, self.sems, self.cols, self.cps = ref, sems, cols, {}

        def go(self, k, a, b, to, rows=pl.ds(0, 96)):
            block = self.ref.at[a, b, rows, self.cols]
            self.cps[k] = send(block, block, self.sems.at[k], to)

        def start_z(self):
            self.go(0, y, zl, dev(dzl=1))

        def start(self):
            for k in range(2):
                self.go(1 + k, y, zl, dev(dy=1 + 2 * k))

        def neighbour(self):
            self.cps[0].wait_recv()
            for k in range(2):
                self.go(3 + k, y, 1 - zl, dev(dy=1 + 2 * k))

        def onward(self, g):
            for k in range(2):
                self.cps[1 + 2 * g + k].wait_recv()
                z = 1 - zl if g else zl
                self.go(5 + 2 * g + k, flip(y, 1 + 2 * k), z, dev(dy=3 - 2 * k), pl.ds(48 * k, 48))

        def finish(self):
            for k in range(5, 9):
                self.cps[k].wait_recv()

    tz = [send(tokf.at[0, 0], tokf.at[e, 0], s_tz.at[e - 1], dev(dzh=e)) for e in (1, 3, 2)]
    wz, wl, wc = [], [], []

    def issue_w(t):
        cp = pltpu.make_async_copy(s_ref.at[zh, :, narrow(t)], wf.at[zh, :, wide(t, c)], s_wl.at[t])
        cp.start()
        wl.append(cp)
        wz.append([
            send(s_ref.at[flip(zh, e), :, narrow(t)], wf.at[zh, :, wide(t, c)],
                 s_wz.at[t], dev(dzh=e))
            for e in (2, 1, 3)
        ])

    def forward_w(t):
        wl[t].wait()
        arrive(wf.at[0:3, :, wide(t, c)], s_wz.at[t])
        wc.append(send(wf.at[:, :, wide(t, c)], wf.at[:, :, wide(t, c)], s_wc.at[t], dev(dc=1)))

    for d in (2, 1, 3):
        send(tokf.at[0, 0], tokf.at[0, d], s_tx.at[0], dev(dx=d))
    stage(1)
    sent(tz)
    issue_w(0)
    stage(2)
    for e, cp in zip((1, 3, 2), tz):
        cp.wait_recv()
        for d in (2, 1, 3):
            send(tokf.at[e, 0], tokf.at[e, d], s_tx.at[0], dev(dx=d))
    stage(3)
    wdl, wdr = [], []
    for t in range(4):
        if t < 3:
            src, at = pl.ds(t * 128, 128), pl.ds(pl.multiple_of(t * 256 + c * 128, 16), 128)
        else:
            src, at = pl.ds(384, 48), pl.ds(pl.multiple_of(768 + c * 48, 16), 48)
        cp = pltpu.make_async_copy(wd_ref.at[src], wdf.at[at], s_wdl.at[t])
        cp.start()
        wdl.append(cp)
        wdr.append(send(wd_ref.at[src], wdf.at[at], s_wd.at[t], dev(dc=1)))
    wdf[864:896, :] = jnp.zeros((32, 640), BF)

    pz = []

    def matmul_pre(t):
        wc[t].wait_recv()
        cols = pl.ds(CO[t], CW[t])
        for f in (2, 1, 3, 0):
            w = wf[:, :, cols].reshape(640, CW[t])
            v = dot(tokf[flip(y, f)].reshape(192, 640), w)
            if f == 2:
                pre_h[:, cols] = v.astype(BF)
                for k in range(2):
                    send(pre_h.at[96 * k : 96 * k + 96, cols], pre_hr.at[k, :, cols], s_ph.at[t], dev(dy=1 + 2 * k))
            elif f:
                pre_f[f // 2, :, cols] = v
            else:
                pre_own[:, cols] = v

    def relay(t):
        cols = pl.ds(CO[t], CW[t])
        arrive(pre_hr.at[:, :, cols], s_ph.at[t])
        pre_s[0, 0:96, cols] = pre_f[0, 0:96, cols].astype(BF)
        pre_s[0, 96:192, cols] = (pre_f[0, 96:192, cols] + pre_hr[1, :, cols].astype(F32)).astype(BF)
        pre_s[1, 0:96, cols] = (pre_f[1, 0:96, cols] + pre_hr[0, :, cols].astype(F32)).astype(BF)
        pre_s[1, 96:192, cols] = pre_f[1, 96:192, cols].astype(BF)
        for k in range(2):
            send(pre_s.at[k, :, cols], pre_r.at[k, :, cols], s_py.at[t], dev(dy=1 + 2 * k))

    def sum_y(t):
        cols = pl.ds(CO[t], CW[t])
        arrive(pre_r.at[:, :, cols], s_py.at[t])

        def half(h):
            rows = pl.ds(pl.multiple_of(h * 96, 16), 96)
            return pre_own[rows, cols] + (pre_r[0, rows, cols].astype(F32) + pre_r[1, rows, cols].astype(F32))

        other = half(1 - zl)
        pre2_s[:, cols] = (other * other * other).astype(BF)
        pz.append(send(pre2_s.at[:, cols], pre2_r.at[:, cols], s_pz.at[t], dev(dzl=1)))
        acc[:, cols] = half(zl)

    lane = lax.broadcasted_iota(jnp.int32, (96, 128), 1)

    def factors(g, u):
        sg = jax.nn.sigmoid(g)
        act = g * sg
        return act * u, u * sg * (1.0 + g * (1.0 - sg)), act

    def finish_pre(t):
        pz[t].wait_recv()
        cols = pl.ds(CO[t], CW[t])
        v = acc[:, cols] + cube_root(pre2_r[:, cols].astype(F32))
        if t < 3:
            for k in range(2):
                h, fa, fb = factors(v[:, k * 256 : k * 256 + 128], v[:, k * 256 + 128 : k * 256 + 256])
                lo = CO[t] + k * 256
                hidf[y, zl, :, t * 256 + k * 128 : t * 256 + k * 128 + 128] = h.astype(BF)
                abf[y, zl, :, lo : lo + 128] = fa.astype(BF)
                abf[y, zl, :, lo + 128 : lo + 256] = fb.astype(BF)
        else:
            hs = []
            for k in range(2):
                g = v[:, k * 128 : k * 128 + 128]
                h, fa, fb = factors(g, pltpu.roll(g, 80, 1))
                hs.append(h)
                lo = CO[3] + k * 128
                abf[y, zl, :, lo : lo + 128] = jnp.where(
                    lane < 48, fa, jnp.where(lane < 96, pltpu.roll(fb, 48, 1), 0.0)
                ).astype(BF)
            tail = jnp.where(lane < 48, hs[0], jnp.where(lane < 96, pltpu.roll(hs[1], 48, 1), 0.0))
            hidf[y, zl, :, 768:896] = tail.astype(BF)

    sent(wz[0])
    issue_w(1)
    forward_w(0)
    arrive(tokf.at[0:3], s_tx.at[0])
    matmul_pre(0)
    sent(wz[1])
    issue_w(2)
    forward_w(1)
    matmul_pre(1)
    relay(0)
    sent(wz[2])
    issue_w(3)
    forward_w(2)
    matmul_pre(2)
    relay(1)
    sum_y(0)
    forward_w(3)
    for e in (2, 1, 3):
        send(cotf.at[0, 0], cotf.at[e, 0], s_cz.at[0], dev(dzh=e))
    matmul_pre(3)
    relay(2)
    sum_y(1)
    relay(3)
    finish_pre(0)
    sum_y(2)
    arrive(cotf.at[0:3, 0], s_cz.at[0])
    for d in (2, 1, 3):
        send(cotf.at[:, 0], cotf.at[:, d], s_cx.at[0], dev(dx=d))
    finish_pre(1)
    hid = [Gather(hidf, s_h, pl.ds(0, 512)), Gather(hidf, s_h2, pl.ds(512, 384))]
    hid[0].start_z()
    sum_y(3)
    hid[0].start()
    finish_pre(2)
    finish_pre(3)

    hid[1].start_z()
    hid[1].start()
    hid[0].neighbour()
    for cp in wdl:
        cp.wait()
    for cp in wdr:
        cp.wait_recv()
    hid[0].onward(0)
    hid[1].neighbour()
    ab = Gather(abf, s_ab, pl.ds(0, 1792))
    ab.start_z()

    def split_x(k, e, v, own_buf, s_buf, r_buf, sem):
        v = v.reshape(4, 48, 640)
        own_buf[e] = v[0]
        s_buf[e] = v[1:4].astype(BF)
        for d in (2, 1, 3):
            send(s_buf.at[e, d - 1], r_buf.at[d - 1, e], sem.at[k], dev(dx=d))

    def total_x(e, own_buf, r_buf):
        return (own_buf[e] + r_buf[0, e].astype(F32)) + (r_buf[1, e].astype(F32) + r_buf[2, e].astype(F32))

    def y_rows(f, e):
        if f == 1:
            hid[0].onward(1)
            hid[1].onward(0)
            hid[1].onward(1)
        elif f == 2:
            hid[0].finish()
            hid[1].finish()
        return dot(hidf[e].reshape(192, 896), wdf[...])

    def after_y():
        ab.start()
        ab.neighbour()

    for k, f in enumerate((0, 1, 3, 2)):
        e = flip(y, f)
        split_x(k, e, y_rows(f, e), y_own, y_s, y_r, s_yx)
    after_y()
    def to_owner(k, e):
        other = ((zh // 2 + e // 2) % 2) * 2 + (zh % 2 + e % 2) % 2
        return pltpu.make_async_remote_copy(
            src_ref=y2_s.at[k], dst_ref=y2_r.at[lax.max(e, 1) - 1], send_sem=s_ys.at[k], recv_sem=s_yz.at[0],
            device_id=(gx, other, gz), device_id_type=pl.DeviceIdType.MESH,
        )

    for k, f in enumerate((0, 1, 3, 2)):
        e = flip(y, f)
        arrive(y_r.at[:, e], s_yx.at[k])
        v = total_x(e, y_own, y_r)
        y2_s[k] = (v * v * v).astype(BF)

        @pl.when(e != 0)
        def _(k=k, e=e):
            to_owner(k, e).start()

    yv = total_x(0, y_own, y_r)
    arrive(y2_r, s_yz.at[0])
    for e in range(3):
        yv = yv + cube_root(y2_r[e].astype(F32))

    sq = yv * yv
    mom[0, 0:4] = jnp.concatenate(
        [jnp.sum(v, 0, keepdims=True) for v in (yv, sq, sq * yv, sq * sq)], 0
    )
    mom[0, 4:8] = jnp.zeros((4, 640), F32)
    for d in (2, 1, 3, 0):
        for k in (1, 0):
            if (d, k) != (0, 0):
                send(mom.at[0], mom_r.at[2 * d + k - 1], s_m.at[0], dev(dx=d, dc=k))
    mxf[0, 0] = (sq * yv).astype(BF)
    mz = [send(mxf.at[0, 0], mxf.at[e, 0], s_gz.at[e - 1], dev(dzh=e)) for e in (1, 3, 2)]
    for d in (2, 1, 3):
        send(mxf.at[0, 0], mxf.at[0, d], s_gx.at[d], dev(dx=d))
    mix[...] = yv.astype(BF)
    outs = [pltpu.make_async_copy(mix, mixed_ref, s_out.at[0])]
    outs[0].start()
    arrive(mom_r.at[0:7], s_m.at[0])
    mom[1] = ((mom[0] + mom_r[0]) + (mom_r[1] + mom_r[2])) + ((mom_r[3] + mom_r[4]) + (mom_r[5] + mom_r[6]))
    for e in (2, 1, 3):
        send(mom.at[1], mom_r.at[6 + e], s_m.at[1], dev(dzh=e))
    for e, cp in zip((1, 3, 2), mz):
        cp.wait_recv()
        for d in (2, 1, 3):
            send(mxf.at[e, 0], mxf.at[e, d], s_gx.at[d], dev(dx=d))
    ab.onward(0)
    ab.onward(1)
    arrive(mom_r.at[7:10], s_m.at[1])
    mom[2] = (mom[1] + mom_r[7]) + (mom_r[8] + mom_r[9])
    arrive(cotf.at[:, 1:4], s_cx.at[0])

    def dh_rows(d):
        if d:
            arrive(mxf.at[:, d], s_gx.at[d])
        totals, weight = mom[2], pw_ref[...].reshape(1, 640)
        for e in range(4):
            gyf[e, d] = penalty_grad(cube_root(mxf[e, d].astype(F32)), totals, cotf[e, d], weight)
        v = dot_t(gyf[:, d].reshape(192, 640), wdf[...])
        dh_s[d // 2, :, (d % 2) * 48 : (d % 2) * 48 + 48, :] = v.astype(BF).reshape(4, 48, 896)

    PART = (pl.ds(512, 384), pl.ds(0, 512))

    def send_rows(d, part):
        p, q = d // 2, d % 2
        rows = pl.ds(48 * q, 48)
        for f in (2, 1, 3):
            send(dh_s.at[p, flip(y, f), rows, PART[part]], dh_r.at[f - 1, zl, rows, PART[part]],
                 s_dh.at[part], dev(dy=f, zl_at=p))

    for d in (0, 1, 3, 2):
        dh_rows(d)
        send_rows(d, 0)
        if d == 0:
            send_rows(0, 1)
    for part in range(2):
        if part:
            for d in (1, 3, 2):
                send_rows(d, 1)
        send(dh_s.at[1 - zl, y, :, PART[part]], dh_p.at[:, PART[part]], s_dhp.at[part], dev(dzl=1))

    def gd_part(core, t):
        if t < 3:
            h = hidf[:, :, :, pl.ds(pl.multiple_of(t * 256 + core * 128, 128), 128)].reshape(768, 128)
        else:
            h = hidf[:, :, :, 768:896].reshape(768, 128)
        return t_dot(h, gyf[...].reshape(768, 640))

    for t in range(3):
        gd_s[t * 128 : t * 128 + 128] = gd_part(1 - c, t).astype(BF)
    gd_acc[384:512] = gd_part(0, 3)
    gd_s[384:432] = gd_acc[pl.ds(pl.multiple_of(384 + (1 - c) * 48, 8), 48)].astype(BF)
    gdc = send(gd_s, gd_r, s_gd.at[0], dev(dc=1))
    for t in range(3):
        gd_acc[t * 128 : t * 128 + 128] = gd_part(c, t)

    HO, HW = (0, 256, 512, 768), (256, 256, 256, 128)
    def sum_dh(t):
        cols = pl.ds(HO[t], HW[t])
        v = dh_s[zl, y, :, cols].astype(F32) + dh_p[:, cols].astype(F32)
        for f in range(3):
            v = v + (dh_r[f, 0, :, cols].astype(F32) + dh_r[f, 1, :, cols].astype(F32))
        dhf[y, zl, :, cols] = v.astype(BF)

    def dh_arrived(part):
        arrive(dh_r.at[:, :, :, PART[part]], s_dh.at[part])
        arrive(dh_p.at[:, PART[part]], s_dhp.at[part])

    direct = {}

    def send_dh(t, sems):
        sum_dh(t)
        own = dhf.at[y, zl, :, pl.ds(HO[t], HW[t])]
        direct[t] = [
            send(own, own, sems.at[2 * f + g - 1], dev(dy=f, dzl=g))
            for f, g in ((2, 1), (2, 0), (1, 1), (3, 1), (1, 0), (3, 0), (0, 1))
        ]

    dh_arrived(0)
    send_dh(3, s_go)
    send_dh(2, s_g2)
    dhg = [Gather(dhf, sems, pl.ds(HO[t], HW[t])) for t, sems in enumerate((s_g0, s_g1))]

    gdc.wait_recv()
    gd_o[0:384] = (gd_acc[0:384] + gd_r[0:384].astype(F32)).astype(BF)
    gd_o[384:432] = (
        gd_acc[pl.ds(pl.multiple_of(384 + c * 48, 8), 48)] + gd_r[384:432].astype(F32)
    ).astype(BF)
    ab.finish()
    outs.append(pltpu.make_async_copy(gd_o, gd_ref, s_out.at[1]))
    outs[1].start()

    dwc, dwl = {}, {}

    def grads_chunk(t):
        if t < 2:
            dhg[t].finish()
        else:
            for cp in direct[t]:
                cp.wait_recv()
        cols = pl.ds(CO[t], CW[t])

        def multiply(i, _):
            e, g = i // 2, i % 2
            if t < 3:
                for k in range(2):
                    dh = dhf[e, g, :, t * 256 + k * 128 : t * 256 + k * 128 + 128].astype(F32)
                    for m in range(2):
                        at = pl.ds(CO[t] + k * 256 + m * 128, 128)
                        dgf[e, g, :, at] = (dh * abf[e, g, :, at].astype(F32)).astype(BF)
            else:
                dh = dhf[e, g, :, 768:896].astype(F32)
                for k in range(2):
                    one = jnp.where(lane < 48, dh if k == 0 else pltpu.roll(dh, 80, 1), 0.0)
                    at = pl.ds(CO[3] + k * 128, 128)
                    both = one + pltpu.roll(one, 48, 1)
                    dgf[e, g, :, at] = (both * abf[e, g, :, at].astype(F32)).astype(BF)
            return 0

        lax.fori_loop(0, 8, multiply, 0)

    def dw_chunk(t):
        nc = CW[t] // 2
        for core, buf in ((1 - c, dw_s), (c, dw_acc)):
            v = t_dot(tokf[...].reshape(768, 640), dgf[:, :, :, wide(t, core)].reshape(768, nc))
            buf[:, narrow(t)] = v.astype(buf.dtype)
            if buf is dw_s:
                dwc[t] = send(dw_s.at[:, narrow(t)], dw_r.at[:, narrow(t)], s_dwc.at[t], dev(dc=1))

    def dt_chunk(t):
        cols = pl.ds(CO[t], CW[t])
        for i in range(2):
            w = wf[:, :, cols].reshape(640, CW[t])
            v = dot_t(dgf[2 * i : 2 * i + 2, :, :, cols].reshape(384, CW[t]), w).reshape(2, 192, 640)
            dt_acc[2 * i : 2 * i + 2] = v if t == 3 else dt_acc[2 * i : 2 * i + 2] + v

    def send_dw(t):
        dwc[t].wait_recv()
        at = narrow(t)
        v = (dw_acc[:, at] + dw_r[:, at].astype(F32)).astype(BF)
        dw_o[:, :, at] = v.reshape(4, 160, v.shape[1])
        cp = pltpu.make_async_copy(dw_o.at[zh, :, at], dw_f.at[zh, :, at], s_wl.at[t])
        cp.start()
        dwl[t] = cp
        for e in (2, 1, 3):
            send(dw_o.at[flip(zh, e), :, at], dw_f.at[zh, :, at], s_dwz.at[t], dev(dzh=e))

    grads_chunk(3)
    dw_chunk(3)
    dh_arrived(1)
    for t in range(2):
        sum_dh(t)
        dhg[t].start_z()
        dhg[t].start()
    dt_chunk(3)
    send_dw(3)
    grads_chunk(2)
    dw_chunk(2)
    dhg[0].neighbour()
    dt_chunk(2)
    send_dw(2)
    dhg[0].onward(0)
    dhg[1].neighbour()
    dhg[0].onward(1)
    dhg[1].onward(0)
    dhg[1].onward(1)
    grads_chunk(0)
    dw_chunk(0)
    dt_chunk(0)
    send_dw(0)
    grads_chunk(1)
    dt_chunk(1)

    for k, e in enumerate((2, 1, 3, 0)):
        split_x(k, e, dt_acc[e], dt_own, dt_s, dt_r, s_dtx)
    dw_chunk(1)
    send_dw(1)
    for k, e in enumerate((2, 1, 3, 0)):
        arrive(dt_r.at[:, e], s_dtx.at[k])
        v = total_x(e, dt_own, dt_r)
        if e:
            dt2_s[e - 1] = v.astype(BF)
            send(dt2_s.at[e - 1], dt2_r.at[e - 1], s_dtz.at[0], dev(dzh=e))
        else:
            dt_own[0] = v
    for t in (3, 2, 0, 1):
        dwl[t].wait()
        arrive(dw_f.at[0:3, :, narrow(t)], s_dwz.at[t])
    for m, out, to in ((0, gw, dg_ref), (1, uw, du_ref)):
        for n in range(14):
            total = None
            for j in range(4):
                for t in range(4):
                    lo = 432 * j + 128 * t
                    size = 128 if t < 3 else 48
                    if lo + size <= 128 * n or lo >= 128 * n + 128:
                        continue
                    at, off = (t * 256 + m * 128, 0) if t < 3 else (768, 48 * m)
                    v = dw_f[j, :, at : at + 128].astype(F32)
                    r = (lo - 128 * n - off) % 128
                    v = pltpu.roll(v, r, 1) if r else v
                    first, last = max(lo - 128 * n, 0), min(lo + size - 128 * n, 128)
                    keep = (lane160 >= first) & (lane160 < last)
                    total = jnp.where(keep, v, 0.0 if total is None else total)
            total = total.astype(BF)
            if n < 13:
                out[:, 128 * n : 128 * n + 128] = total
            else:
                out[:, 1664:1728] = total[:, 0:64]
        outs.append(pltpu.make_async_copy(out, to, s_out.at[3 + m]))
        outs[-1].start()
    arrive(dt2_r, s_dtz.at[0])
    dt_o[...] = ((dt_own[0] + dt2_r[0].astype(F32)) + (dt2_r[1].astype(F32) + dt2_r[2].astype(F32))).astype(BF)
    outs.append(pltpu.make_async_copy(dt_o, dtok_ref, s_out.at[2]))
    outs[-1].start()
    for cp in outs:
        cp.wait()
    for k, f in enumerate((0, 1, 3, 2)):
        e = flip(y, f)

        @pl.when(e != 0)
        def _(k=k, e=e):
            to_owner(k, e).wait_send()

    for cp in pending.values():
        cp.wait_send()


def hand_over(*refs):
    ins = [pltpu.make_async_copy(refs[k], refs[10 + k], refs[15].at[k]) for k in range(5)]
    outs = [pltpu.make_async_copy(refs[10 + k], refs[5 + k], refs[16].at[k]) for k in range(5)]
    for cp in ins:
        cp.start()
    for k in range(5):
        ins[k].wait()
        outs[k].start()
    for cp in outs:
        cp.wait()


def body(tokens, gate_weight, up_weight, down_weight, cotangent, penalty_weight):
    V, D = pltpu.VMEM, pltpu.SemaphoreType.DMA
    scratch = [
        V((160, 1728), BF), V((160, 1728), BF), V((48, 640), BF), V((48, 640), BF), V((432, 640), BF), V((4, 160, 896), BF),
        V((4, 160, 1792), BF), V((4, 4, 48, 640), BF), V((192, 1792), BF), V((2, 96, 1792), BF), V((2, 192, 1792), F32),
        V((2, 192, 1792), BF), V((2, 192, 1792), BF),
        V((192, 1792), F32), V((96, 1792), F32), V((96, 1792), BF), V((96, 1792), BF),
        V((4, 2, 96, 1792), BF), V((4, 2, 96, 896), BF), V((896, 640), BF),
        V((4, 48, 640), F32), V((4, 3, 48, 640), BF), V((3, 4, 48, 640), BF), V((4, 48, 640), BF), V((3, 48, 640), BF),
        V((3, 8, 640), F32), V((10, 8, 640), F32), V((4, 4, 48, 640), BF), V((4, 4, 48, 640), BF), V((4, 4, 48, 640), BF),
        V((2, 4, 96, 896), BF), V((3, 2, 96, 896), BF), V((96, 896), BF),
        V((512, 640), F32), V((432, 640), BF), V((432, 640), BF), V((4, 2, 96, 896), BF),
        V((4, 2, 96, 1792), BF), V((4, 192, 640), F32),
        V((4, 48, 640), F32), V((4, 3, 48, 640), BF), V((3, 4, 48, 640), BF), V((3, 48, 640), BF), V((3, 48, 640), BF),
        V((640, 896), F32), V((640, 896), BF), V((640, 896), BF), V((4, 160, 896), BF), V((4, 160, 896), BF),
        D((SLOTS,)), D((4,)), D((5,)), D((3,)), D((1,)), D((4,)), D((4,)), D((4,)), D((4,)), D((4,)), D((4,)), D((9,)), D((9,)),
        D((4,)), D((4,)), D((4,)), D((1,)), D((4,)), D((2,)),
        D((3,)), D((4,)), D((1,)), D((1,)), D((9,)),
        D((2,)), D((2,)), D((1,)), D((7,)), D((9,)), D((9,)), D((7,)),
        D((4,)), D((1,)), D((4,)), D((4,)),
    ]
    S = jax.ShapeDtypeStruct
    in_vmem = pl.BlockSpec(memory_space=pltpu.VMEM)
    in_any = pl.BlockSpec(memory_space=pl.ANY)
    shapes = [S((48, 640), BF), S((48, 640), BF), S((160, 1728), BF), S((160, 1728), BF), S((432, 640), BF)]
    results = pl.pallas_call(
        kernel,
        out_shape=shapes,
        in_specs=[in_any] * 5 + [in_vmem],
        out_specs=[in_any] * 5,
        scratch_shapes=scratch,
        compiler_params=pltpu.CompilerParams(
            collective_id=0, has_side_effects=True, vmem_limit_bytes=58 * 2**20
        ),
        cost_estimate=pl.CostEstimate(flops=8 * 10**9, bytes_accessed=6 * 10**6, transcendentals=0),
        name="ffn",
    )(gate_weight, up_weight, tokens, down_weight, cotangent, penalty_weight)
    return tuple(
        pl.pallas_call(
            hand_over,
            out_shape=shapes,
            in_specs=[in_any] * 5,
            out_specs=[in_any] * 5,
            scratch_shapes=[V(a.shape, BF) for a in shapes] + [D((5,)), D((5,))],
            name="hand_over",
        )(*results)
    )


def solution(mesh):
    in_specs = (
        P(("gy", "gx"), "gz"),
        P(("gz", "gy"), "gx"),
        P(("gz", "gy"), "gx"),
        P(("gx", "gy"), "gz"),
        P(("gy", "gx"), "gz"),
        P("gz"),
    )
    out_specs = (
        P(("gy", "gx"), "gz"),
        P(("gy", "gx"), "gz"),
        P(("gz", "gy"), "gx"),
        P(("gz", "gy"), "gx"),
        P(("gx", "gy"), "gz"),
    )
    return jax.shard_map(body, mesh=mesh, in_specs=in_specs, out_specs=out_specs, check_vma=False)
```

```python
import jax
import jax.numpy as jnp
from jax import lax
from jax.experimental import pallas as pl
from jax.experimental.pallas import tpu as pltpu
from jax.sharding import PartitionSpec as P

EPSILON = 1e-05
BF, F32 = jnp.bfloat16, jnp.float32
NT = 1536.0
CO = (0, 512, 1024, 1536)
CW = (512, 512, 512, 256)
SLOTS = 48


def dot(a, b):
    return lax.dot_general(a, b, (((1,), (0,)), ((), ())), preferred_element_type=F32)


def dot_t(a, b):
    return lax.dot_general(a, b, (((1,), (1,)), ((), ())), preferred_element_type=F32)


def t_dot(a, b):
    return lax.dot_general(a, b, (((0,), (0,)), ((), ())), preferred_element_type=F32)


def penalty_grad(values, totals, cotangent, weight):
    mean = totals[0:1] / NT
    two = totals[1:2] / NT
    three = totals[2:3] / NT
    four = totals[3:4] / NT
    c2 = two - mean * mean
    c3 = three - 3.0 * mean * two + 2.0 * mean * mean * mean
    c4 = four - 4.0 * mean * three + 6.0 * mean * mean * two - 3.0 * mean * mean * mean * mean
    v = c2 + EPSILON
    d = values - mean
    extra = (d * d * d - c3) / (v * v) - c4 * d / (v * v * v)
    return (cotangent.astype(F32) + weight * extra).astype(BF)


def cube_root(q):
    r = jnp.exp(jnp.log(jnp.abs(q)) * (1.0 / 3.0))
    return jnp.where(q < 0.0, -r, r)


def wide(t, core):
    if t < 3:
        return pl.ds(pl.multiple_of(CO[t] + core * 256, 128), 256)
    return pl.ds(pl.multiple_of(CO[3] + core * 128, 128), 128)


def narrow(t):
    return pl.ds(t * 256, 256 if t < 3 else 128)


def kernel(
    gw_ref, uw_ref, tok_ref, wd_ref, cot_ref, pw_ref,
    mixed_ref, dtok_ref, dg_ref, du_ref, gd_ref,
    gw, uw, mix, dt_o, gd_o, s_ref, wf, tokf, pre_h, pre_hr, pre_f, pre_s, pre_r, pre_own, acc, pre2_s, pre2_r,
    abf, hidf, wdf, y_own, y_s, y_r, y2_s, y2_r, mom, mom_r, mxf, cotf, gyf,
    dh_s, dh_r, dh_p, gd_acc, gd_s, gd_r, dhf,
    dgf, dt_acc, dt_own, dt_s, dt_r, dt2_s, dt2_r, dw_acc, dw_s, dw_r, dw_o, dw_f,
    s_send, s_in, s_out, s_tz, s_tx, s_wz, s_wl, s_wc, s_ph, s_py, s_pz, s_h, s_h2, s_wd, s_wdl, s_yx, s_yz, s_ys, s_m,
    s_gz, s_gx, s_cz, s_cx, s_ab, s_dh, s_dhp, s_gd, s_go, s_g0, s_g1, s_g2, s_dtx, s_dtz, s_dwc, s_dwz,
):
    gx, gy, gz = lax.axis_index("gx"), lax.axis_index("gy"), lax.axis_index("gz")
    x, c, zh, y, zl = gx // 2, gx % 2, gy, gz // 2, gz % 2

    def flip(a, k):
        if k == 1:
            return a + 1 - 2 * (a % 2)
        if k == 2:
            return (a + 2) % 4
        if k == 3:
            return 3 - a
        return a

    def dev(dx=0, dc=0, dy=0, dzh=0, dzl=0, zl_at=None):
        zz = zl_at if zl_at is not None else (1 - zl if dzl else zl)
        cc = 1 - c if dc else c
        return (flip(x, dx) * 2 + cc, flip(zh, dzh), flip(y, dy) * 2 + zz)

    pending, started = {}, [0]

    def send(src, dst, rs, to):
        slot = started[0] % SLOTS
        started[0] += 1
        if slot in pending:
            pending.pop(slot).wait_send()
        cp = pltpu.make_async_remote_copy(
            src_ref=src, dst_ref=dst, send_sem=s_send.at[slot], recv_sem=rs,
            device_id=to, device_id_type=pl.DeviceIdType.MESH,
        )
        cp.start()
        pending[slot] = cp
        return cp

    def arrive(ref, sem):
        pltpu.make_async_remote_copy(
            src_ref=ref, dst_ref=ref, send_sem=s_send.at[0], recv_sem=sem,
            device_id=dev(dc=1), device_id_type=pl.DeviceIdType.MESH,
        ).wait_recv()

    def sent(cps):
        for slot in [k for k, cp in pending.items() if any(cp is other for other in cps)]:
            pending.pop(slot).wait_send()

    barrier = pltpu.get_barrier_semaphore()
    peers = [dev(dx=d, dc=k) for d in range(4) for k in range(2) if (d, k) != (0, 0)]
    peers += [dev(dzh=e) for e in (1, 2, 3)]
    peers += [dev(dy=f, dzl=g) for f in range(4) for g in range(2) if (f, g) != (0, 0)]
    for p in peers:
        pl.semaphore_signal(barrier, inc=1, device_id=p, device_id_type=pl.DeviceIdType.MESH)
    ins = [
        pltpu.make_async_copy(src, to, s_in.at[k])
        for k, (src, to) in enumerate(((tok_ref, tokf.at[0, 0]), (gw_ref, gw), (uw_ref, uw), (cot_ref, cotf.at[0, 0])))
    ]
    for cp in ins:
        cp.start()
    lane160 = lax.broadcasted_iota(jnp.int32, (160, 128), 1)

    def shifted(ref, lo, at):
        base = lo // 128 * 128
        v = ref[:, base : min(base + 256, 1728)].astype(F32)
        if v.shape[1] < 256:
            v = jnp.concatenate([v, jnp.zeros((160, 256 - v.shape[1]), F32)], 1)
        r = (at - (lo - base)) % 256
        return (pltpu.roll(v, r, 1) if r else v)[:, 0:128]

    def stage(t):
        for j in range(4):
            if t < 3:
                for k, ref in enumerate((gw, uw)):
                    s_ref[j, :, t * 256 + k * 128 : t * 256 + k * 128 + 128] = shifted(ref, 432 * j + 128 * t, 0).astype(BF)
            else:
                g, u = shifted(gw, 432 * j + 384, 0), shifted(uw, 432 * j + 384, 48)
                s_ref[j, :, 768:896] = jnp.where(lane160 < 48, g, jnp.where(lane160 < 96, u, 0.0)).astype(BF)

    for cp in ins:
        cp.wait()
    stage(0)
    pl.semaphore_wait(barrier, len(peers))

    class Gather:
        def __init__(self, ref, sems, cols):
            self.ref, self.sems, self.cols, self.cps = ref, sems, cols, {}

        def go(self, k, a, b, to, rows=pl.ds(0, 96)):
            block = self.ref.at[a, b, rows, self.cols]
            self.cps[k] = send(block, block, self.sems.at[k], to)

        def start_z(self):
            self.go(0, y, zl, dev(dzl=1))

        def start(self):
            for k in range(2):
                self.go(1 + k, y, zl, dev(dy=1 + 2 * k))

        def neighbour(self):
            self.cps[0].wait_recv()
            for k in range(2):
                self.go(3 + k, y, 1 - zl, dev(dy=1 + 2 * k))

        def onward(self, g):
            for k in range(2):
                self.cps[1 + 2 * g + k].wait_recv()
                z = 1 - zl if g else zl
                self.go(5 + 2 * g + k, flip(y, 1 + 2 * k), z, dev(dy=3 - 2 * k), pl.ds(48 * k, 48))

        def finish(self):
            for k in range(5, 9):
                self.cps[k].wait_recv()

    tz = [send(tokf.at[0, 0], tokf.at[e, 0], s_tz.at[e - 1], dev(dzh=e)) for e in (1, 3, 2)]
    wz, wl = [], []

    def issue_w(t):
        cp = pltpu.make_async_copy(s_ref.at[zh, :, narrow(t)], wf.at[zh, :, wide(t, c)], s_wl.at[t])
        cp.start()
        wl.append(cp)
        wz.append([
            send(s_ref.at[flip(zh, e), :, narrow(t)], wf.at[zh, :, wide(t, c)],
                 s_wz.at[t, 1 if e == 2 else 0], dev(dzh=e))
            for e in (2, 1, 3)
        ])

    def forward_w(t):
        cols = wide(t, c)

        def forward(e):
            piece = wf.at[flip(zh, e), :, cols]
            send(piece, piece, s_wc.at[t], dev(dc=1))

        wl[t].wait()
        forward(0)
        arrive(wf.at[0:2, :, cols], s_wz.at[t, 0])
        forward(1)
        forward(3)
        arrive(wf.at[0, :, cols], s_wz.at[t, 1])
        forward(2)

    for d in (2, 1, 3):
        send(tokf.at[0, 0], tokf.at[0, d], s_tx.at[0], dev(dx=d))
    stage(1)
    sent(tz)
    issue_w(0)
    stage(2)
    for e, cp in zip((1, 3, 2), tz):
        cp.wait_recv()
        for d in (2, 1, 3):
            send(tokf.at[e, 0], tokf.at[e, d], s_tx.at[0], dev(dx=d))
    stage(3)
    wdl, wdr = [], []
    for t in range(4):
        if t < 3:
            src, at = pl.ds(t * 128, 128), pl.ds(pl.multiple_of(t * 256 + c * 128, 16), 128)
        else:
            src, at = pl.ds(384, 48), pl.ds(pl.multiple_of(768 + c * 48, 16), 48)
        cp = pltpu.make_async_copy(wd_ref.at[src], wdf.at[at], s_wdl.at[t])
        cp.start()
        wdl.append(cp)
        wdr.append(send(wd_ref.at[src], wdf.at[at], s_wd.at[t], dev(dc=1)))
    wdf[864:896, :] = jnp.zeros((32, 640), BF)

    pz = []

    def matmul_pre(t):
        cols = pl.ds(CO[t], CW[t])
        arrive(wf.at[:, :, wide(t, 1 - c)], s_wc.at[t])
        for f in (2, 1, 3, 0):
            w = wf[:, :, cols].reshape(640, CW[t])
            v = dot(tokf[flip(y, f)].reshape(192, 640), w)
            if f == 2:
                pre_h[:, cols] = v.astype(BF)
                for k in range(2):
                    send(pre_h.at[96 * k : 96 * k + 96, cols], pre_hr.at[k, :, cols], s_ph.at[t], dev(dy=1 + 2 * k))
            elif f:
                pre_f[f // 2, :, cols] = v
            else:
                pre_own[:, cols] = v

    def relay(t):
        cols = pl.ds(CO[t], CW[t])
        arrive(pre_hr.at[:, :, cols], s_ph.at[t])
        pre_s[0, 0:96, cols] = pre_f[0, 0:96, cols].astype(BF)
        pre_s[0, 96:192, cols] = (pre_f[0, 96:192, cols] + pre_hr[1, :, cols].astype(F32)).astype(BF)
        pre_s[1, 0:96, cols] = (pre_f[1, 0:96, cols] + pre_hr[0, :, cols].astype(F32)).astype(BF)
        pre_s[1, 96:192, cols] = pre_f[1, 96:192, cols].astype(BF)
        for k in range(2):
            send(pre_s.at[k, :, cols], pre_r.at[k, :, cols], s_py.at[t], dev(dy=1 + 2 * k))

    def sum_y(t):
        cols = pl.ds(CO[t], CW[t])
        arrive(pre_r.at[:, :, cols], s_py.at[t])

        def half(h):
            rows = pl.ds(pl.multiple_of(h * 96, 16), 96)
            return pre_own[rows, cols] + (pre_r[0, rows, cols].astype(F32) + pre_r[1, rows, cols].astype(F32))

        other = half(1 - zl)
        pre2_s[:, cols] = (other * other * other).astype(BF)
        pz.append(send(pre2_s.at[:, cols], pre2_r.at[:, cols], s_pz.at[t], dev(dzl=1)))
        acc[:, cols] = half(zl)

    lane = lax.broadcasted_iota(jnp.int32, (96, 128), 1)

    def factors(g, u):
        sg = jax.nn.sigmoid(g)
        act = g * sg
        return act * u, u * sg * (1.0 + g * (1.0 - sg)), act

    def finish_pre(t):
        pz[t].wait_recv()
        cols = pl.ds(CO[t], CW[t])
        v = acc[:, cols] + cube_root(pre2_r[:, cols].astype(F32))
        if t < 3:
            for k in range(2):
                h, fa, fb = factors(v[:, k * 256 : k * 256 + 128], v[:, k * 256 + 128 : k * 256 + 256])
                lo = CO[t] + k * 256
                hidf[y, zl, :, t * 256 + k * 128 : t * 256 + k * 128 + 128] = h.astype(BF)
                abf[y, zl, :, lo : lo + 128] = fa.astype(BF)
                abf[y, zl, :, lo + 128 : lo + 256] = fb.astype(BF)
        else:
            hs = []
            for k in range(2):
                g = v[:, k * 128 : k * 128 + 128]
                h, fa, fb = factors(g, pltpu.roll(g, 80, 1))
                hs.append(h)
                lo = CO[3] + k * 128
                abf[y, zl, :, lo : lo + 128] = jnp.where(
                    lane < 48, fa, jnp.where(lane < 96, pltpu.roll(fb, 48, 1), 0.0)
                ).astype(BF)
            tail = jnp.where(lane < 48, hs[0], jnp.where(lane < 96, pltpu.roll(hs[1], 48, 1), 0.0))
            hidf[y, zl, :, 768:896] = tail.astype(BF)

    sent(wz[0])
    issue_w(1)
    forward_w(0)
    arrive(tokf.at[0:3], s_tx.at[0])
    matmul_pre(0)
    sent(wz[1])
    issue_w(2)
    forward_w(1)
    matmul_pre(1)
    relay(0)
    sent(wz[2])
    issue_w(3)
    forward_w(2)
    relay(1)
    matmul_pre(2)
    sum_y(0)
    forward_w(3)
    for e in (2, 1, 3):
        send(cotf.at[0, 0], cotf.at[e, 0], s_cz.at[0], dev(dzh=e))
    matmul_pre(3)
    relay(2)
    sum_y(1)
    relay(3)
    finish_pre(0)
    sum_y(2)
    arrive(cotf.at[0:3, 0], s_cz.at[0])
    for d in (2, 1, 3):
        send(cotf.at[:, 0], cotf.at[:, d], s_cx.at[0], dev(dx=d))
    finish_pre(1)
    hid = [Gather(hidf, s_h, pl.ds(0, 512)), Gather(hidf, s_h2, pl.ds(512, 384))]
    hid[0].start_z()
    sum_y(3)
    hid[0].start()
    finish_pre(2)
    finish_pre(3)

    hid[1].start_z()
    hid[1].start()
    hid[0].neighbour()
    for cp in wdl:
        cp.wait()
    for cp in wdr:
        cp.wait_recv()
    hid[0].onward(0)
    hid[1].neighbour()
    ab = Gather(abf, s_ab, pl.ds(1024, 768))
    ab.start_z()

    def split_x(k, e, v, own_buf, s_buf, r_buf, sem):
        v = v.reshape(4, 48, 640)
        own_buf[e] = v[0]
        s_buf[e] = v[1:4].astype(BF)
        for d in (2, 1, 3):
            send(s_buf.at[e, d - 1], r_buf.at[d - 1, e], sem.at[k], dev(dx=d))

    def total_x(e, own_buf, r_buf):
        return (own_buf[e] + r_buf[0, e].astype(F32)) + (r_buf[1, e].astype(F32) + r_buf[2, e].astype(F32))

    def y_rows(f, e):
        if f == 1:
            hid[0].onward(1)
            hid[1].onward(0)
            hid[1].onward(1)
        elif f == 2:
            hid[0].finish()
            hid[1].finish()
        return dot(hidf[e].reshape(192, 896), wdf[...])

    def after_y():
        ab.start()
        ab.neighbour()

    for k, f in enumerate((0, 1, 3, 2)):
        e = flip(y, f)
        split_x(k, e, y_rows(f, e), y_own, y_s, y_r, s_yx)
    after_y()
    def to_owner(k, e):
        other = ((zh // 2 + e // 2) % 2) * 2 + (zh % 2 + e % 2) % 2
        return pltpu.make_async_remote_copy(
            src_ref=y2_s.at[k], dst_ref=y2_r.at[lax.max(e, 1) - 1], send_sem=s_ys.at[k], recv_sem=s_yz.at[0],
            device_id=(gx, other, gz), device_id_type=pl.DeviceIdType.MESH,
        )

    for k, f in enumerate((0, 1, 3, 2)):
        e = flip(y, f)
        arrive(y_r.at[:, e], s_yx.at[k])
        v = total_x(e, y_own, y_r)
        y2_s[k] = (v * v * v).astype(BF)

        @pl.when(e != 0)
        def _(k=k, e=e):
            to_owner(k, e).start()

    yv = total_x(0, y_own, y_r)
    arrive(y2_r, s_yz.at[0])
    for e in range(3):
        yv = yv + cube_root(y2_r[e].astype(F32))

    sq = yv * yv
    mom[0, 0:4] = jnp.concatenate(
        [jnp.sum(v, 0, keepdims=True) for v in (yv, sq, sq * yv, sq * sq)], 0
    )
    mom[0, 4:8] = jnp.zeros((4, 640), F32)
    for d in (2, 1, 3, 0):
        for k in (1, 0):
            if (d, k) != (0, 0):
                send(mom.at[0], mom_r.at[2 * d + k - 1], s_m.at[0], dev(dx=d, dc=k))
    mxf[0, 0] = (sq * yv).astype(BF)
    mz = [send(mxf.at[0, 0], mxf.at[e, 0], s_gz.at[e - 1], dev(dzh=e)) for e in (1, 3, 2)]
    for d in (2, 1, 3):
        send(mxf.at[0, 0], mxf.at[0, d], s_gx.at[d], dev(dx=d))
    mix[...] = yv.astype(BF)
    outs = [pltpu.make_async_copy(mix, mixed_ref, s_out.at[0])]
    outs[0].start()
    ab.onward(0)
    ab.onward(1)
    arrive(mom_r.at[0:7], s_m.at[0])
    mom[1] = ((mom[0] + mom_r[0]) + (mom_r[1] + mom_r[2])) + ((mom_r[3] + mom_r[4]) + (mom_r[5] + mom_r[6]))
    for e in (2, 1, 3):
        send(mom.at[1], mom_r.at[6 + e], s_m.at[1], dev(dzh=e))
    for e, cp in zip((1, 3, 2), mz):
        cp.wait_recv()
        for d in (2, 1, 3):
            send(mxf.at[e, 0], mxf.at[e, d], s_gx.at[d], dev(dx=d))
    arrive(mom_r.at[7:10], s_m.at[1])
    mom[2] = (mom[1] + mom_r[7]) + (mom_r[8] + mom_r[9])
    arrive(cotf.at[:, 1:4], s_cx.at[0])

    def dh_rows(d):
        if d:
            arrive(mxf.at[:, d], s_gx.at[d])
        totals, weight = mom[2], pw_ref[...].reshape(1, 640)
        for e in range(4):
            gyf[e, d] = penalty_grad(cube_root(mxf[e, d].astype(F32)), totals, cotf[e, d], weight)
        v = dot_t(gyf[:, d].reshape(192, 640), wdf[...])
        dh_s[d // 2, :, (d % 2) * 48 : (d % 2) * 48 + 48, :] = v.astype(BF).reshape(4, 48, 896)

    PART = (pl.ds(512, 384), pl.ds(0, 512))

    def send_rows(d, part):
        p, q = d // 2, d % 2
        rows = pl.ds(48 * q, 48)
        for f in (2, 1, 3):
            send(dh_s.at[p, flip(y, f), rows, PART[part]], dh_r.at[f - 1, zl, rows, PART[part]],
                 s_dh.at[part], dev(dy=f, zl_at=p))

    for d in (0, 1, 3, 2):
        dh_rows(d)
        send_rows(d, 0)
        if d == 0:
            send_rows(0, 1)
    for part in range(2):
        if part:
            for d in (1, 3, 2):
                send_rows(d, 1)
        send(dh_s.at[1 - zl, y, :, PART[part]], dh_p.at[:, PART[part]], s_dhp.at[part], dev(dzl=1))

    def gd_part(core, t):
        if t < 3:
            h = hidf[:, :, :, pl.ds(pl.multiple_of(t * 256 + core * 128, 128), 128)].reshape(768, 128)
        else:
            h = hidf[:, :, :, 768:896].reshape(768, 128)
        return t_dot(h, gyf[...].reshape(768, 640))

    for t in range(3):
        gd_s[t * 128 : t * 128 + 128] = gd_part(1 - c, t).astype(BF)
    gd_acc[384:512] = gd_part(0, 3)
    gd_s[384:432] = gd_acc[pl.ds(pl.multiple_of(384 + (1 - c) * 48, 8), 48)].astype(BF)
    gdc = send(gd_s, gd_r, s_gd.at[0], dev(dc=1))
    for t in range(3):
        gd_acc[t * 128 : t * 128 + 128] = gd_part(c, t)

    HO, HW = (0, 256, 512, 768), (256, 256, 256, 128)
    def total_dh(cols):
        v = dh_s[zl, y, :, cols].astype(F32) + dh_p[:, cols].astype(F32)
        for f in range(3):
            v = v + (dh_r[f, 0, :, cols].astype(F32) + dh_r[f, 1, :, cols].astype(F32))
        return v

    def own_grads(t):
        for k in range(2):
            dh = total_dh(pl.ds(HO[t] + k * 128, 128))
            for m in range(2):
                at = pl.ds(CO[t] + k * 256 + m * 128, 128)
                dgf[y, zl, :, at] = (dh * abf[y, zl, :, at].astype(F32)).astype(BF)

    def dh_arrived(part):
        arrive(dh_r.at[:, :, :, PART[part]], s_dh.at[part])
        arrive(dh_p.at[:, PART[part]], s_dhp.at[part])

    direct = {}

    def send_dh(t, sems):
        cols = pl.ds(HO[t], HW[t])
        dhf[y, zl, :, cols] = total_dh(cols).astype(BF)
        own = dhf.at[y, zl, :, cols]
        direct[t] = [
            send(own, own, sems.at[2 * f + g - 1], dev(dy=f, dzl=g))
            for f, g in ((2, 1), (2, 0), (1, 1), (3, 1), (1, 0), (3, 0), (0, 1))
        ]

    dh_arrived(0)
    send_dh(3, s_go)
    send_dh(2, s_g2)
    dhg = [Gather(dgf, sems, pl.ds(CO[t], CW[t])) for t, sems in enumerate((s_g0, s_g1))]

    gdc.wait_recv()
    gd_o[0:384] = (gd_acc[0:384] + gd_r[0:384].astype(F32)).astype(BF)
    gd_o[384:432] = (
        gd_acc[pl.ds(pl.multiple_of(384 + c * 48, 8), 48)] + gd_r[384:432].astype(F32)
    ).astype(BF)
    ab.finish()
    outs.append(pltpu.make_async_copy(gd_o, gd_ref, s_out.at[1]))
    outs[1].start()

    dwc, dwl = {}, {}

    def grads_chunk(t):
        if t < 2:
            dhg[t].finish()
            return
        for cp in direct[t]:
            cp.wait_recv()

        def multiply(i, _):
            e, g = i // 2, i % 2
            if t < 3:
                for k in range(2):
                    dh = dhf[e, g, :, t * 256 + k * 128 : t * 256 + k * 128 + 128].astype(F32)
                    for m in range(2):
                        at = pl.ds(CO[t] + k * 256 + m * 128, 128)
                        dgf[e, g, :, at] = (dh * abf[e, g, :, at].astype(F32)).astype(BF)
            else:
                dh = dhf[e, g, :, 768:896].astype(F32)
                for k in range(2):
                    one = jnp.where(lane < 48, dh if k == 0 else pltpu.roll(dh, 80, 1), 0.0)
                    at = pl.ds(CO[3] + k * 128, 128)
                    both = one + pltpu.roll(one, 48, 1)
                    dgf[e, g, :, at] = (both * abf[e, g, :, at].astype(F32)).astype(BF)
            return 0

        lax.fori_loop(0, 8, multiply, 0)

    def dw_chunk(t):
        nc = CW[t] // 2
        for core, buf in ((1 - c, dw_s), (c, dw_acc)):
            v = t_dot(tokf[...].reshape(768, 640), dgf[:, :, :, wide(t, core)].reshape(768, nc))
            buf[:, narrow(t)] = v.astype(buf.dtype)
            if buf is dw_s:
                dwc[t] = send(dw_s.at[:, narrow(t)], dw_r.at[:, narrow(t)], s_dwc.at[t], dev(dc=1))

    def dt_chunk(t):
        cols = pl.ds(CO[t], CW[t])
        for i in range(2):
            w = wf[:, :, cols].reshape(640, CW[t])
            v = dot_t(dgf[2 * i : 2 * i + 2, :, :, cols].reshape(384, CW[t]), w).reshape(2, 192, 640)
            dt_acc[2 * i : 2 * i + 2] = v if t == 3 else dt_acc[2 * i : 2 * i + 2] + v

    def send_dw(t):
        dwc[t].wait_recv()
        at = narrow(t)
        v = (dw_acc[:, at] + dw_r[:, at].astype(F32)).astype(BF)
        dw_o[:, :, at] = v.reshape(4, 160, v.shape[1])
        cp = pltpu.make_async_copy(dw_o.at[zh, :, at], dw_f.at[zh, :, at], s_wl.at[t])
        cp.start()
        dwl[t] = cp
        for e in (2, 1, 3):
            send(dw_o.at[flip(zh, e), :, at], dw_f.at[zh, :, at], s_dwz.at[t], dev(dzh=e))

    dh_arrived(1)
    for t in range(2):
        own_grads(t)
        dhg[t].start_z()
        dhg[t].start()
    grads_chunk(3)
    dw_chunk(3)
    dt_chunk(3)
    send_dw(3)
    grads_chunk(2)
    dw_chunk(2)
    dhg[0].neighbour()
    dt_chunk(2)
    send_dw(2)
    dhg[0].onward(0)
    dhg[1].neighbour()
    dhg[0].onward(1)
    dhg[1].onward(0)
    dhg[1].onward(1)
    grads_chunk(0)
    dw_chunk(0)
    dt_chunk(0)
    send_dw(0)
    grads_chunk(1)
    dt_chunk(1)

    for k, e in enumerate((2, 1, 3, 0)):
        split_x(k, e, dt_acc[e], dt_own, dt_s, dt_r, s_dtx)
    dw_chunk(1)
    send_dw(1)
    for k, e in enumerate((2, 1, 3, 0)):
        arrive(dt_r.at[:, e], s_dtx.at[k])
        v = total_x(e, dt_own, dt_r)
        if e:
            dt2_s[e - 1] = v.astype(BF)
            send(dt2_s.at[e - 1], dt2_r.at[e - 1], s_dtz.at[0], dev(dzh=e))
        else:
            dt_own[0] = v
    for t in (3, 2, 0, 1):
        dwl[t].wait()
        arrive(dw_f.at[0:3, :, narrow(t)], s_dwz.at[t])
    for m, out, to in ((0, gw, dg_ref), (1, uw, du_ref)):
        for n in range(14):
            total = None
            for j in range(4):
                for t in range(4):
                    lo = 432 * j + 128 * t
                    size = 128 if t < 3 else 48
                    if lo + size <= 128 * n or lo >= 128 * n + 128:
                        continue
                    at, off = (t * 256 + m * 128, 0) if t < 3 else (768, 48 * m)
                    v = dw_f[j, :, at : at + 128].astype(F32)
                    r = (lo - 128 * n - off) % 128
                    v = pltpu.roll(v, r, 1) if r else v
                    first, last = max(lo - 128 * n, 0), min(lo + size - 128 * n, 128)
                    keep = (lane160 >= first) & (lane160 < last)
                    total = jnp.where(keep, v, 0.0 if total is None else total)
            total = total.astype(BF)
            if n < 13:
                out[:, 128 * n : 128 * n + 128] = total
            else:
                out[:, 1664:1728] = total[:, 0:64]
        outs.append(pltpu.make_async_copy(out, to, s_out.at[3 + m]))
        outs[-1].start()
    arrive(dt2_r, s_dtz.at[0])
    dt_o[...] = ((dt_own[0] + dt2_r[0].astype(F32)) + (dt2_r[1].astype(F32) + dt2_r[2].astype(F32))).astype(BF)
    outs.append(pltpu.make_async_copy(dt_o, dtok_ref, s_out.at[2]))
    outs[-1].start()
    for cp in outs:
        cp.wait()
    for k, f in enumerate((0, 1, 3, 2)):
        e = flip(y, f)

        @pl.when(e != 0)
        def _(k=k, e=e):
            to_owner(k, e).wait_send()

    for cp in pending.values():
        cp.wait_send()


def hand_over(*refs):
    ins = [pltpu.make_async_copy(refs[k], refs[10 + k], refs[15].at[k]) for k in range(5)]
    outs = [pltpu.make_async_copy(refs[10 + k], refs[5 + k], refs[16].at[k]) for k in range(5)]
    for cp in ins:
        cp.start()
    for k in range(5):
        ins[k].wait()
        outs[k].start()
    for cp in outs:
        cp.wait()


def body(tokens, gate_weight, up_weight, down_weight, cotangent, penalty_weight):
    V, D = pltpu.VMEM, pltpu.SemaphoreType.DMA
    scratch = [
        V((160, 1728), BF), V((160, 1728), BF), V((48, 640), BF), V((48, 640), BF), V((432, 640), BF), V((4, 160, 896), BF),
        V((4, 160, 1792), BF), V((4, 4, 48, 640), BF), V((192, 1792), BF), V((2, 96, 1792), BF), V((2, 192, 1792), F32),
        V((2, 192, 1792), BF), V((2, 192, 1792), BF),
        V((192, 1792), F32), V((96, 1792), F32), V((96, 1792), BF), V((96, 1792), BF),
        V((4, 2, 96, 1792), BF), V((4, 2, 96, 896), BF), V((896, 640), BF),
        V((4, 48, 640), F32), V((4, 3, 48, 640), BF), V((3, 4, 48, 640), BF), V((4, 48, 640), BF), V((3, 48, 640), BF),
        V((3, 8, 640), F32), V((10, 8, 640), F32), V((4, 4, 48, 640), BF), V((4, 4, 48, 640), BF), V((4, 4, 48, 640), BF),
        V((2, 4, 96, 896), BF), V((3, 2, 96, 896), BF), V((96, 896), BF),
        V((512, 640), F32), V((432, 640), BF), V((432, 640), BF), V((4, 2, 96, 896), BF),
        V((4, 2, 96, 1792), BF), V((4, 192, 640), F32),
        V((4, 48, 640), F32), V((4, 3, 48, 640), BF), V((3, 4, 48, 640), BF), V((3, 48, 640), BF), V((3, 48, 640), BF),
        V((640, 896), F32), V((640, 896), BF), V((640, 896), BF), V((4, 160, 896), BF), V((4, 160, 896), BF),
        D((SLOTS,)), D((4,)), D((5,)), D((3,)), D((1,)), D((4, 2)), D((4,)), D((4,)), D((4,)), D((4,)), D((4,)), D((9,)), D((9,)),
        D((4,)), D((4,)), D((4,)), D((1,)), D((4,)), D((2,)),
        D((3,)), D((4,)), D((1,)), D((1,)), D((9,)),
        D((2,)), D((2,)), D((1,)), D((7,)), D((9,)), D((9,)), D((7,)),
        D((4,)), D((1,)), D((4,)), D((4,)),
    ]
    S = jax.ShapeDtypeStruct
    in_vmem = pl.BlockSpec(memory_space=pltpu.VMEM)
    in_any = pl.BlockSpec(memory_space=pl.ANY)
    shapes = [S((48, 640), BF), S((48, 640), BF), S((160, 1728), BF), S((160, 1728), BF), S((432, 640), BF)]
    results = pl.pallas_call(
        kernel,
        out_shape=shapes,
        in_specs=[in_any] * 5 + [in_vmem],
        out_specs=[in_any] * 5,
        scratch_shapes=scratch,
        compiler_params=pltpu.CompilerParams(
            collective_id=0, has_side_effects=True, vmem_limit_bytes=58 * 2**20
        ),
        cost_estimate=pl.CostEstimate(flops=8 * 10**9, bytes_accessed=6 * 10**6, transcendentals=0),
        name="ffn",
    )(gate_weight, up_weight, tokens, down_weight, cotangent, penalty_weight)
    return tuple(
        pl.pallas_call(
            hand_over,
            out_shape=shapes,
            in_specs=[in_any] * 5,
            out_specs=[in_any] * 5,
            scratch_shapes=[V(a.shape, BF) for a in shapes] + [D((5,)), D((5,))],
            name="hand_over",
        )(*results)
    )


def solution(mesh):
    in_specs = (
        P(("gy", "gx"), "gz"),
        P(("gz", "gy"), "gx"),
        P(("gz", "gy"), "gx"),
        P(("gx", "gy"), "gz"),
        P(("gy", "gx"), "gz"),
        P("gz"),
    )
    out_specs = (
        P(("gy", "gx"), "gz"),
        P(("gy", "gx"), "gz"),
        P(("gz", "gy"), "gx"),
        P(("gz", "gy"), "gx"),
        P(("gx", "gy"), "gz"),
    )
    return jax.shard_map(body, mesh=mesh, in_specs=in_specs, out_specs=out_specs, check_vma=False)
```

```python
import jax
import jax.numpy as jnp
from jax import lax
from jax.experimental import pallas as pl
from jax.experimental.pallas import tpu as pltpu
from jax.sharding import PartitionSpec as P

EPSILON = 1e-05
BF, F32 = jnp.bfloat16, jnp.float32
NT = 1536.0
CO = (0, 512, 1024, 1536)
CW = (512, 512, 512, 256)
SLOTS = 48


def dot(a, b):
    return lax.dot_general(a, b, (((1,), (0,)), ((), ())), preferred_element_type=F32)


def dot_t(a, b):
    return lax.dot_general(a, b, (((1,), (1,)), ((), ())), preferred_element_type=F32)


def t_dot(a, b):
    return lax.dot_general(a, b, (((0,), (0,)), ((), ())), preferred_element_type=F32)


def penalty_grad(values, totals, cotangent, weight):
    mean = totals[0:1] / NT
    two = totals[1:2] / NT
    three = totals[2:3] / NT
    four = totals[3:4] / NT
    c2 = two - mean * mean
    c3 = three - 3.0 * mean * two + 2.0 * mean * mean * mean
    c4 = four - 4.0 * mean * three + 6.0 * mean * mean * two - 3.0 * mean * mean * mean * mean
    v = c2 + EPSILON
    d = values - mean
    extra = (d * d * d - c3) / (v * v) - c4 * d / (v * v * v)
    return (cotangent.astype(F32) + weight * extra).astype(BF)


def cube_root(q):
    r = jnp.exp(jnp.log(jnp.abs(q)) * (1.0 / 3.0))
    return jnp.where(q < 0.0, -r, r)


def wide(t, core):
    if t < 3:
        return pl.ds(pl.multiple_of(CO[t] + core * 256, 128), 256)
    return pl.ds(pl.multiple_of(CO[3] + core * 128, 128), 128)


def narrow(t):
    return pl.ds(t * 256, 256 if t < 3 else 128)


def kernel(
    gw_ref, uw_ref, tok_ref, wd_ref, cot_ref, pw_ref,
    mixed_ref, dtok_ref, dg_ref, du_ref, gd_ref,
    gw, uw, mix, dt_o, gd_o, s_ref, wf, tokf, pre_h, pre_hr, pre_f, pre_s, pre_r, pre_own, acc, pre2_s, pre2_r,
    abf, hidf, wdf, y_own, y_s, y_r, y2_s, y2_r, mom, mom_r, mxf, cotf, gyf,
    dh_s, dh_r, dh_p, gd_acc, gd_s, gd_r, dhf,
    dgf, dt_acc, dt_own, dt_s, dt_r, dt2_s, dt2_r, dw_acc, dw_s, dw_r, dw_o, dw_f,
    s_send, s_in, s_out, s_tz, s_tx, s_wz, s_wl, s_wc, s_ph, s_py, s_pz, s_h, s_h2, s_h3, s_wd, s_wdl, s_yx, s_yz, s_ys, s_m,
    s_gz, s_gx, s_cz, s_cx, s_ab, s_dh, s_dhp, s_gd, s_go, s_g0, s_g1, s_g2, s_dtx, s_dtz, s_dwc, s_dwz,
):
    gx, gy, gz = lax.axis_index("gx"), lax.axis_index("gy"), lax.axis_index("gz")
    x, c, zh, y, zl = gx // 2, gx % 2, gy, gz // 2, gz % 2

    def flip(a, k):
        if k == 1:
            return a + 1 - 2 * (a % 2)
        if k == 2:
            return (a + 2) % 4
        if k == 3:
            return 3 - a
        return a

    def dev(dx=0, dc=0, dy=0, dzh=0, dzl=0, zl_at=None):
        zz = zl_at if zl_at is not None else (1 - zl if dzl else zl)
        cc = 1 - c if dc else c
        return (flip(x, dx) * 2 + cc, flip(zh, dzh), flip(y, dy) * 2 + zz)

    pending, started = {}, [0]

    def send(src, dst, rs, to):
        slot = started[0] % SLOTS
        started[0] += 1
        if slot in pending:
            pending.pop(slot).wait_send()
        cp = pltpu.make_async_remote_copy(
            src_ref=src, dst_ref=dst, send_sem=s_send.at[slot], recv_sem=rs,
            device_id=to, device_id_type=pl.DeviceIdType.MESH,
        )
        cp.start()
        pending[slot] = cp
        return cp

    def arrive(ref, sem):
        pltpu.make_async_remote_copy(
            src_ref=ref, dst_ref=ref, send_sem=s_send.at[0], recv_sem=sem,
            device_id=dev(dc=1), device_id_type=pl.DeviceIdType.MESH,
        ).wait_recv()

    def sent(cps):
        for slot in [k for k, cp in pending.items() if any(cp is other for other in cps)]:
            pending.pop(slot).wait_send()

    barrier = pltpu.get_barrier_semaphore()
    peers = [dev(dx=d, dc=k) for d in range(4) for k in range(2) if (d, k) != (0, 0)]
    peers += [dev(dzh=e) for e in (1, 2, 3)]
    peers += [dev(dy=f, dzl=g) for f in range(4) for g in range(2) if (f, g) != (0, 0)]
    for p in peers:
        pl.semaphore_signal(barrier, inc=1, device_id=p, device_id_type=pl.DeviceIdType.MESH)
    ins = [
        pltpu.make_async_copy(src, to, s_in.at[k])
        for k, (src, to) in enumerate(((tok_ref, tokf.at[0, 0]), (gw_ref, gw), (uw_ref, uw), (cot_ref, cotf.at[0, 0])))
    ]
    for cp in ins:
        cp.start()
    lane160 = lax.broadcasted_iota(jnp.int32, (160, 128), 1)

    def shifted(ref, lo, at):
        base = lo // 128 * 128
        v = ref[:, base : min(base + 256, 1728)].astype(F32)
        if v.shape[1] < 256:
            v = jnp.concatenate([v, jnp.zeros((160, 256 - v.shape[1]), F32)], 1)
        r = (at - (lo - base)) % 256
        return (pltpu.roll(v, r, 1) if r else v)[:, 0:128]

    def stage(t):
        for j in range(4):
            if t < 3:
                for k, ref in enumerate((gw, uw)):
                    s_ref[j, :, t * 256 + k * 128 : t * 256 + k * 128 + 128] = shifted(ref, 432 * j + 128 * t, 0).astype(BF)
            else:
                g, u = shifted(gw, 432 * j + 384, 0), shifted(uw, 432 * j + 384, 48)
                s_ref[j, :, 768:896] = jnp.where(lane160 < 48, g, jnp.where(lane160 < 96, u, 0.0)).astype(BF)

    for cp in ins:
        cp.wait()
    stage(0)
    pl.semaphore_wait(barrier, len(peers))

    class Gather:
        def __init__(self, ref, sems, cols):
            self.ref, self.sems, self.cols, self.cps = ref, sems, cols, {}

        def go(self, k, a, b, to, rows=pl.ds(0, 96)):
            block = self.ref.at[a, b, rows, self.cols]
            self.cps[k] = send(block, block, self.sems.at[k], to)

        def start_z(self):
            self.go(0, y, zl, dev(dzl=1))

        def start(self):
            for k in range(2):
                self.go(1 + k, y, zl, dev(dy=1 + 2 * k))

        def neighbour(self):
            self.cps[0].wait_recv()
            for k in range(2):
                self.go(3 + k, y, 1 - zl, dev(dy=1 + 2 * k))

        def onward(self, g):
            for k in range(2):
                self.cps[1 + 2 * g + k].wait_recv()
                z = 1 - zl if g else zl
                self.go(5 + 2 * g + k, flip(y, 1 + 2 * k), z, dev(dy=3 - 2 * k), pl.ds(48 * k, 48))

        def finish(self):
            for k in range(5, 9):
                self.cps[k].wait_recv()

    tz = [send(tokf.at[0, 0], tokf.at[e, 0], s_tz.at[e - 1], dev(dzh=e)) for e in (1, 3, 2)]
    wz, wl = [], []

    def issue_w(t):
        cp = pltpu.make_async_copy(s_ref.at[zh, :, narrow(t)], wf.at[zh, :, wide(t, c)], s_wl.at[t])
        cp.start()
        wl.append(cp)
        wz.append([
            send(s_ref.at[flip(zh, e), :, narrow(t)], wf.at[zh, :, wide(t, c)],
                 s_wz.at[t, 1 if e == 2 else 0], dev(dzh=e))
            for e in (2, 1, 3)
        ])

    def forward_w(t):
        cols = wide(t, c)

        def forward(e):
            piece = wf.at[flip(zh, e), :, cols]
            send(piece, piece, s_wc.at[t], dev(dc=1))

        wl[t].wait()
        forward(0)
        arrive(wf.at[0:2, :, cols], s_wz.at[t, 0])
        forward(1)
        forward(3)
        arrive(wf.at[0, :, cols], s_wz.at[t, 1])
        forward(2)

    for d in (2, 1, 3):
        send(tokf.at[0, 0], tokf.at[0, d], s_tx.at[0], dev(dx=d))
    stage(1)
    sent(tz)
    issue_w(0)
    stage(2)
    for e, cp in zip((1, 3, 2), tz):
        cp.wait_recv()
        for d in (2, 1, 3):
            send(tokf.at[e, 0], tokf.at[e, d], s_tx.at[0], dev(dx=d))
    stage(3)
    wdl, wdr = [], []
    for t in range(4):
        if t < 3:
            src, at = pl.ds(t * 128, 128), pl.ds(pl.multiple_of(t * 256 + c * 128, 16), 128)
        else:
            src, at = pl.ds(384, 48), pl.ds(pl.multiple_of(768 + c * 48, 16), 48)
        cp = pltpu.make_async_copy(wd_ref.at[src], wdf.at[at], s_wdl.at[t])
        cp.start()
        wdl.append(cp)
        wdr.append(send(wd_ref.at[src], wdf.at[at], s_wd.at[t], dev(dc=1)))
    wdf[864:896, :] = jnp.zeros((32, 640), BF)

    pz = []

    def matmul_pre(t):
        cols = pl.ds(CO[t], CW[t])
        arrive(wf.at[:, :, wide(t, 1 - c)], s_wc.at[t])
        for f in (2, 1, 3, 0):
            w = wf[:, :, cols].reshape(640, CW[t])
            v = dot(tokf[flip(y, f)].reshape(192, 640), w)
            if f == 2:
                pre_h[:, cols] = v.astype(BF)
                for k in range(2):
                    send(pre_h.at[96 * k : 96 * k + 96, cols], pre_hr.at[k, :, cols], s_ph.at[t], dev(dy=1 + 2 * k))
            elif f:
                pre_f[f // 2, :, cols] = v
            else:
                pre_own[:, cols] = v

    def relay(t):
        cols = pl.ds(CO[t], CW[t])
        arrive(pre_hr.at[:, :, cols], s_ph.at[t])
        pre_s[0, 0:96, cols] = pre_f[0, 0:96, cols].astype(BF)
        pre_s[0, 96:192, cols] = (pre_f[0, 96:192, cols] + pre_hr[1, :, cols].astype(F32)).astype(BF)
        pre_s[1, 0:96, cols] = (pre_f[1, 0:96, cols] + pre_hr[0, :, cols].astype(F32)).astype(BF)
        pre_s[1, 96:192, cols] = pre_f[1, 96:192, cols].astype(BF)
        for k in range(2):
            send(pre_s.at[k, :, cols], pre_r.at[k, :, cols], s_py.at[t], dev(dy=1 + 2 * k))

    def sum_y(t):
        cols = pl.ds(CO[t], CW[t])
        arrive(pre_r.at[:, :, cols], s_py.at[t])

        def half(h):
            rows = pl.ds(pl.multiple_of(h * 96, 16), 96)
            return pre_own[rows, cols] + (pre_r[0, rows, cols].astype(F32) + pre_r[1, rows, cols].astype(F32))

        other = half(1 - zl)
        pre2_s[:, cols] = (other * other * other).astype(BF)
        pz.append(send(pre2_s.at[:, cols], pre2_r.at[:, cols], s_pz.at[t], dev(dzl=1)))
        acc[:, cols] = half(zl)

    lane = lax.broadcasted_iota(jnp.int32, (96, 128), 1)

    def factors(g, u):
        sg = jax.nn.sigmoid(g)
        act = g * sg
        return act * u, u * sg * (1.0 + g * (1.0 - sg)), act

    def finish_pre(t):
        pz[t].wait_recv()
        cols = pl.ds(CO[t], CW[t])
        v = acc[:, cols] + cube_root(pre2_r[:, cols].astype(F32))
        if t < 3:
            for k in range(2):
                h, fa, fb = factors(v[:, k * 256 : k * 256 + 128], v[:, k * 256 + 128 : k * 256 + 256])
                lo = CO[t] + k * 256
                hidf[y, zl, :, t * 256 + k * 128 : t * 256 + k * 128 + 128] = h.astype(BF)
                abf[y, zl, :, lo : lo + 128] = fa.astype(BF)
                abf[y, zl, :, lo + 128 : lo + 256] = fb.astype(BF)
        else:
            hs = []
            for k in range(2):
                g = v[:, k * 128 : k * 128 + 128]
                h, fa, fb = factors(g, pltpu.roll(g, 80, 1))
                hs.append(h)
                lo = CO[3] + k * 128
                abf[y, zl, :, lo : lo + 128] = jnp.where(
                    lane < 48, fa, jnp.where(lane < 96, pltpu.roll(fb, 48, 1), 0.0)
                ).astype(BF)
            tail = jnp.where(lane < 48, hs[0], jnp.where(lane < 96, pltpu.roll(hs[1], 48, 1), 0.0))
            hidf[y, zl, :, 768:896] = tail.astype(BF)

    sent(wz[0])
    issue_w(1)
    forward_w(0)
    arrive(tokf.at[0:3], s_tx.at[0])
    matmul_pre(0)
    sent(wz[1])
    issue_w(2)
    forward_w(1)
    matmul_pre(1)
    relay(0)
    sent(wz[2])
    issue_w(3)
    forward_w(2)
    relay(1)
    matmul_pre(2)
    sum_y(0)
    forward_w(3)
    for e in (2, 1, 3):
        send(cotf.at[0, 0], cotf.at[e, 0], s_cz.at[0], dev(dzh=e))
    matmul_pre(3)
    relay(2)
    sum_y(1)
    relay(3)
    finish_pre(0)
    sum_y(2)
    arrive(cotf.at[0:3, 0], s_cz.at[0])
    for d in (2, 1, 3):
        send(cotf.at[:, 0], cotf.at[:, d], s_cx.at[0], dev(dx=d))
    finish_pre(1)
    hid = [Gather(hidf, sems, pl.ds(lo, n)) for sems, lo, n in ((s_h, 0, 512), (s_h2, 512, 256), (s_h3, 768, 128))]
    hid[0].start_z()
    sum_y(3)
    hid[0].start()
    finish_pre(2)
    hid[1].start_z()
    hid[1].start()
    hid[0].neighbour()
    finish_pre(3)

    hid[2].start_z()
    hid[2].start()
    for cp in wdl:
        cp.wait()
    for cp in wdr:
        cp.wait_recv()
    hid[1].neighbour()
    hid[0].onward(0)
    hid[2].neighbour()
    ab = Gather(abf, s_ab, pl.ds(1024, 768))
    ab.start_z()

    def split_x(k, e, v, own_buf, s_buf, r_buf, sem):
        v = v.reshape(4, 48, 640)
        own_buf[e] = v[0]
        s_buf[e] = v[1:4].astype(BF)
        for d in (2, 1, 3):
            send(s_buf.at[e, d - 1], r_buf.at[d - 1, e], sem.at[k], dev(dx=d))

    def total_x(e, own_buf, r_buf):
        return (own_buf[e] + r_buf[0, e].astype(F32)) + (r_buf[1, e].astype(F32) + r_buf[2, e].astype(F32))

    def y_rows(f, e):
        if f == 1:
            hid[0].onward(1)
            hid[1].onward(0)
            hid[1].onward(1)
            hid[2].onward(0)
            hid[2].onward(1)
        elif f == 2:
            hid[0].finish()
            hid[1].finish()
            hid[2].finish()
        return dot(hidf[e].reshape(192, 896), wdf[...])

    def after_y():
        ab.start()
        ab.neighbour()

    for k, f in enumerate((0, 1, 3, 2)):
        e = flip(y, f)
        split_x(k, e, y_rows(f, e), y_own, y_s, y_r, s_yx)
    after_y()
    def to_owner(k, e):
        other = ((zh // 2 + e // 2) % 2) * 2 + (zh % 2 + e % 2) % 2
        return pltpu.make_async_remote_copy(
            src_ref=y2_s.at[k], dst_ref=y2_r.at[lax.max(e, 1) - 1], send_sem=s_ys.at[k], recv_sem=s_yz.at[0],
            device_id=(gx, other, gz), device_id_type=pl.DeviceIdType.MESH,
        )

    for k, f in enumerate((0, 1, 3, 2)):
        e = flip(y, f)
        arrive(y_r.at[:, e], s_yx.at[k])
        v = total_x(e, y_own, y_r)
        y2_s[k] = (v * v * v).astype(BF)

        @pl.when(e != 0)
        def _(k=k, e=e):
            to_owner(k, e).start()

    yv = total_x(0, y_own, y_r)
    arrive(y2_r, s_yz.at[0])
    for e in range(3):
        yv = yv + cube_root(y2_r[e].astype(F32))

    sq = yv * yv
    mom[0, 0:4] = jnp.concatenate(
        [jnp.sum(v, 0, keepdims=True) for v in (yv, sq, sq * yv, sq * sq)], 0
    )
    mom[0, 4:8] = jnp.zeros((4, 640), F32)
    for d in (2, 1, 3, 0):
        for k in (1, 0):
            if (d, k) != (0, 0):
                send(mom.at[0], mom_r.at[2 * d + k - 1], s_m.at[0], dev(dx=d, dc=k))
    mxf[0, 0] = (sq * yv).astype(BF)
    mz = [send(mxf.at[0, 0], mxf.at[e, 0], s_gz.at[e - 1], dev(dzh=e)) for e in (1, 3, 2)]
    for d in (2, 1, 3):
        send(mxf.at[0, 0], mxf.at[0, d], s_gx.at[d], dev(dx=d))
    mix[...] = yv.astype(BF)
    outs = [pltpu.make_async_copy(mix, mixed_ref, s_out.at[0])]
    outs[0].start()
    ab.onward(0)
    ab.onward(1)
    arrive(mom_r.at[0:7], s_m.at[0])
    mom[1] = ((mom[0] + mom_r[0]) + (mom_r[1] + mom_r[2])) + ((mom_r[3] + mom_r[4]) + (mom_r[5] + mom_r[6]))
    for e in (2, 1, 3):
        send(mom.at[1], mom_r.at[6 + e], s_m.at[1], dev(dzh=e))
    for e, cp in zip((1, 3, 2), mz):
        cp.wait_recv()
        for d in (2, 1, 3):
            send(mxf.at[e, 0], mxf.at[e, d], s_gx.at[d], dev(dx=d))
    arrive(mom_r.at[7:10], s_m.at[1])
    mom[2] = (mom[1] + mom_r[7]) + (mom_r[8] + mom_r[9])
    arrive(cotf.at[:, 1:4], s_cx.at[0])

    def dh_rows(d):
        if d:
            arrive(mxf.at[:, d], s_gx.at[d])
        totals, weight = mom[2], pw_ref[...].reshape(1, 640)
        for e in range(4):
            gyf[e, d] = penalty_grad(cube_root(mxf[e, d].astype(F32)), totals, cotf[e, d], weight)
        v = dot_t(gyf[:, d].reshape(192, 640), wdf[...])
        dh_s[d // 2, :, (d % 2) * 48 : (d % 2) * 48 + 48, :] = v.astype(BF).reshape(4, 48, 896)

    PART = (pl.ds(512, 384), pl.ds(0, 512))

    def send_rows(d, part):
        p, q = d // 2, d % 2
        rows = pl.ds(48 * q, 48)
        for f in (2, 1, 3):
            send(dh_s.at[p, flip(y, f), rows, PART[part]], dh_r.at[f - 1, zl, rows, PART[part]],
                 s_dh.at[part], dev(dy=f, zl_at=p))

    for d in (0, 1, 3, 2):
        dh_rows(d)
        send_rows(d, 0)
        if d == 0:
            send_rows(0, 1)
    for part in range(2):
        if part:
            for d in (1, 3, 2):
                send_rows(d, 1)
        send(dh_s.at[1 - zl, y, :, PART[part]], dh_p.at[:, PART[part]], s_dhp.at[part], dev(dzl=1))

    def gd_part(core, t):
        if t < 3:
            h = hidf[:, :, :, pl.ds(pl.multiple_of(t * 256 + core * 128, 128), 128)].reshape(768, 128)
        else:
            h = hidf[:, :, :, 768:896].reshape(768, 128)
        return t_dot(h, gyf[...].reshape(768, 640))

    for t in range(3):
        gd_s[t * 128 : t * 128 + 128] = gd_part(1 - c, t).astype(BF)
    gd_acc[384:512] = gd_part(0, 3)
    gd_s[384:432] = gd_acc[pl.ds(pl.multiple_of(384 + (1 - c) * 48, 8), 48)].astype(BF)
    gdc = send(gd_s, gd_r, s_gd.at[0], dev(dc=1))
    for t in range(3):
        gd_acc[t * 128 : t * 128 + 128] = gd_part(c, t)

    HO, HW = (0, 256, 512, 768), (256, 256, 256, 128)
    def total_dh(cols):
        v = dh_s[zl, y, :, cols].astype(F32) + dh_p[:, cols].astype(F32)
        for f in range(3):
            v = v + (dh_r[f, 0, :, cols].astype(F32) + dh_r[f, 1, :, cols].astype(F32))
        return v

    def own_grads(t):
        for k in range(2):
            dh = total_dh(pl.ds(HO[t] + k * 128, 128))
            for m in range(2):
                at = pl.ds(CO[t] + k * 256 + m * 128, 128)
                dgf[y, zl, :, at] = (dh * abf[y, zl, :, at].astype(F32)).astype(BF)

    def dh_arrived(part):
        arrive(dh_r.at[:, :, :, PART[part]], s_dh.at[part])
        arrive(dh_p.at[:, PART[part]], s_dhp.at[part])

    direct = {}

    def send_dh(t, sems):
        cols = pl.ds(HO[t], HW[t])
        dhf[y, zl, :, cols] = total_dh(cols).astype(BF)
        own = dhf.at[y, zl, :, cols]
        direct[t] = [
            send(own, own, sems.at[2 * f + g - 1], dev(dy=f, dzl=g))
            for f, g in ((2, 1), (2, 0), (1, 1), (3, 1), (1, 0), (3, 0), (0, 1))
        ]

    dh_arrived(0)
    send_dh(3, s_go)
    send_dh(2, s_g2)
    dhg = [Gather(dgf, sems, pl.ds(CO[t], CW[t])) for t, sems in enumerate((s_g0, s_g1))]

    gdc.wait_recv()
    gd_o[0:384] = (gd_acc[0:384] + gd_r[0:384].astype(F32)).astype(BF)
    gd_o[384:432] = (
        gd_acc[pl.ds(pl.multiple_of(384 + c * 48, 8), 48)] + gd_r[384:432].astype(F32)
    ).astype(BF)
    ab.finish()
    outs.append(pltpu.make_async_copy(gd_o, gd_ref, s_out.at[1]))
    outs[1].start()

    dwc, dwl = {}, {}

    def grads_chunk(t):
        if t < 2:
            dhg[t].finish()
            return
        for cp in direct[t]:
            cp.wait_recv()

        def multiply(i, _):
            e, g = i // 2, i % 2
            if t < 3:
                for k in range(2):
                    dh = dhf[e, g, :, t * 256 + k * 128 : t * 256 + k * 128 + 128].astype(F32)
                    for m in range(2):
                        at = pl.ds(CO[t] + k * 256 + m * 128, 128)
                        dgf[e, g, :, at] = (dh * abf[e, g, :, at].astype(F32)).astype(BF)
            else:
                dh = dhf[e, g, :, 768:896].astype(F32)
                for k in range(2):
                    one = jnp.where(lane < 48, dh if k == 0 else pltpu.roll(dh, 80, 1), 0.0)
                    at = pl.ds(CO[3] + k * 128, 128)
                    both = one + pltpu.roll(one, 48, 1)
                    dgf[e, g, :, at] = (both * abf[e, g, :, at].astype(F32)).astype(BF)
            return 0

        lax.fori_loop(0, 8, multiply, 0)

    def dw_chunk(t):
        nc = CW[t] // 2
        for core, buf in ((1 - c, dw_s), (c, dw_acc)):
            v = t_dot(tokf[...].reshape(768, 640), dgf[:, :, :, wide(t, core)].reshape(768, nc))
            buf[:, narrow(t)] = v.astype(buf.dtype)
            if buf is dw_s:
                dwc[t] = send(dw_s.at[:, narrow(t)], dw_r.at[:, narrow(t)], s_dwc.at[t], dev(dc=1))

    def dt_chunk(t):
        cols = pl.ds(CO[t], CW[t])
        for i in range(2):
            w = wf[:, :, cols].reshape(640, CW[t])
            v = dot_t(dgf[2 * i : 2 * i + 2, :, :, cols].reshape(384, CW[t]), w).reshape(2, 192, 640)
            dt_acc[2 * i : 2 * i + 2] = v if t == 3 else dt_acc[2 * i : 2 * i + 2] + v

    def send_dw(t):
        dwc[t].wait_recv()
        at = narrow(t)
        v = (dw_acc[:, at] + dw_r[:, at].astype(F32)).astype(BF)
        dw_o[:, :, at] = v.reshape(4, 160, v.shape[1])
        cp = pltpu.make_async_copy(dw_o.at[zh, :, at], dw_f.at[zh, :, at], s_wl.at[t])
        cp.start()
        dwl[t] = cp
        for e in (2, 1, 3):
            send(dw_o.at[flip(zh, e), :, at], dw_f.at[zh, :, at], s_dwz.at[t], dev(dzh=e))

    dh_arrived(1)
    for t in range(2):
        own_grads(t)
        dhg[t].start_z()
        dhg[t].start()
    grads_chunk(3)
    dw_chunk(3)
    dt_chunk(3)
    send_dw(3)
    grads_chunk(2)
    dw_chunk(2)
    dhg[0].neighbour()
    dt_chunk(2)
    send_dw(2)
    dhg[0].onward(0)
    dhg[1].neighbour()
    dhg[0].onward(1)
    dhg[1].onward(0)
    dhg[1].onward(1)
    grads_chunk(0)
    dw_chunk(0)
    dt_chunk(0)
    send_dw(0)
    grads_chunk(1)
    dt_chunk(1)

    for k, e in enumerate((2, 1, 3, 0)):
        split_x(k, e, dt_acc[e], dt_own, dt_s, dt_r, s_dtx)
    dw_chunk(1)
    send_dw(1)
    for k, e in enumerate((2, 1, 3, 0)):
        arrive(dt_r.at[:, e], s_dtx.at[k])
        v = total_x(e, dt_own, dt_r)
        if e:
            dt2_s[e - 1] = v.astype(BF)
            send(dt2_s.at[e - 1], dt2_r.at[e - 1], s_dtz.at[0], dev(dzh=e))
        else:
            dt_own[0] = v
    for t in (3, 2, 0, 1):
        dwl[t].wait()
        arrive(dw_f.at[0:3, :, narrow(t)], s_dwz.at[t])
    for m, out, to in ((0, gw, dg_ref), (1, uw, du_ref)):
        for n in range(14):
            total = None
            for j in range(4):
                for t in range(4):
                    lo = 432 * j + 128 * t
                    size = 128 if t < 3 else 48
                    if lo + size <= 128 * n or lo >= 128 * n + 128:
                        continue
                    at, off = (t * 256 + m * 128, 0) if t < 3 else (768, 48 * m)
                    v = dw_f[j, :, at : at + 128].astype(F32)
                    r = (lo - 128 * n - off) % 128
                    v = pltpu.roll(v, r, 1) if r else v
                    first, last = max(lo - 128 * n, 0), min(lo + size - 128 * n, 128)
                    keep = (lane160 >= first) & (lane160 < last)
                    total = jnp.where(keep, v, 0.0 if total is None else total)
            total = total.astype(BF)
            if n < 13:
                out[:, 128 * n : 128 * n + 128] = total
            else:
                out[:, 1664:1728] = total[:, 0:64]
        outs.append(pltpu.make_async_copy(out, to, s_out.at[3 + m]))
        outs[-1].start()
    arrive(dt2_r, s_dtz.at[0])
    dt_o[...] = ((dt_own[0] + dt2_r[0].astype(F32)) + (dt2_r[1].astype(F32) + dt2_r[2].astype(F32))).astype(BF)
    outs.append(pltpu.make_async_copy(dt_o, dtok_ref, s_out.at[2]))
    outs[-1].start()
    for cp in outs:
        cp.wait()
    for k, f in enumerate((0, 1, 3, 2)):
        e = flip(y, f)

        @pl.when(e != 0)
        def _(k=k, e=e):
            to_owner(k, e).wait_send()

    for cp in pending.values():
        cp.wait_send()


def hand_over(*refs):
    ins = [pltpu.make_async_copy(refs[k], refs[10 + k], refs[15].at[k]) for k in range(5)]
    outs = [pltpu.make_async_copy(refs[10 + k], refs[5 + k], refs[16].at[k]) for k in range(5)]
    for cp in ins:
        cp.start()
    for k in range(5):
        ins[k].wait()
        outs[k].start()
    for cp in outs:
        cp.wait()


def body(tokens, gate_weight, up_weight, down_weight, cotangent, penalty_weight):
    V, D = pltpu.VMEM, pltpu.SemaphoreType.DMA
    scratch = [
        V((160, 1728), BF), V((160, 1728), BF), V((48, 640), BF), V((48, 640), BF), V((432, 640), BF), V((4, 160, 896), BF),
        V((4, 160, 1792), BF), V((4, 4, 48, 640), BF), V((192, 1792), BF), V((2, 96, 1792), BF), V((2, 192, 1792), F32),
        V((2, 192, 1792), BF), V((2, 192, 1792), BF),
        V((192, 1792), F32), V((96, 1792), F32), V((96, 1792), BF), V((96, 1792), BF),
        V((4, 2, 96, 1792), BF), V((4, 2, 96, 896), BF), V((896, 640), BF),
        V((4, 48, 640), F32), V((4, 3, 48, 640), BF), V((3, 4, 48, 640), BF), V((4, 48, 640), BF), V((3, 48, 640), BF),
        V((3, 8, 640), F32), V((10, 8, 640), F32), V((4, 4, 48, 640), BF), V((4, 4, 48, 640), BF), V((4, 4, 48, 640), BF),
        V((2, 4, 96, 896), BF), V((3, 2, 96, 896), BF), V((96, 896), BF),
        V((512, 640), F32), V((432, 640), BF), V((432, 640), BF), V((4, 2, 96, 896), BF),
        V((4, 2, 96, 1792), BF), V((4, 192, 640), F32),
        V((4, 48, 640), F32), V((4, 3, 48, 640), BF), V((3, 4, 48, 640), BF), V((3, 48, 640), BF), V((3, 48, 640), BF),
        V((640, 896), F32), V((640, 896), BF), V((640, 896), BF), V((4, 160, 896), BF), V((4, 160, 896), BF),
        D((SLOTS,)), D((4,)), D((5,)), D((3,)), D((1,)), D((4, 2)), D((4,)), D((4,)), D((4,)), D((4,)), D((4,)), D((9,)), D((9,)), D((9,)),
        D((4,)), D((4,)), D((4,)), D((1,)), D((4,)), D((2,)),
        D((3,)), D((4,)), D((1,)), D((1,)), D((9,)),
        D((2,)), D((2,)), D((1,)), D((7,)), D((9,)), D((9,)), D((7,)),
        D((4,)), D((1,)), D((4,)), D((4,)),
    ]
    S = jax.ShapeDtypeStruct
    in_vmem = pl.BlockSpec(memory_space=pltpu.VMEM)
    in_any = pl.BlockSpec(memory_space=pl.ANY)
    shapes = [S((48, 640), BF), S((48, 640), BF), S((160, 1728), BF), S((160, 1728), BF), S((432, 640), BF)]
    results = pl.pallas_call(
        kernel,
        out_shape=shapes,
        in_specs=[in_any] * 5 + [in_vmem],
        out_specs=[in_any] * 5,
        scratch_shapes=scratch,
        compiler_params=pltpu.CompilerParams(
            collective_id=0, has_side_effects=True, vmem_limit_bytes=58 * 2**20
        ),
        cost_estimate=pl.CostEstimate(flops=8 * 10**9, bytes_accessed=6 * 10**6, transcendentals=0),
        name="ffn",
    )(gate_weight, up_weight, tokens, down_weight, cotangent, penalty_weight)
    return tuple(
        pl.pallas_call(
            hand_over,
            out_shape=shapes,
            in_specs=[in_any] * 5,
            out_specs=[in_any] * 5,
            scratch_shapes=[V(a.shape, BF) for a in shapes] + [D((5,)), D((5,))],
            name="hand_over",
        )(*results)
    )


def solution(mesh):
    in_specs = (
        P(("gy", "gx"), "gz"),
        P(("gz", "gy"), "gx"),
        P(("gz", "gy"), "gx"),
        P(("gx", "gy"), "gz"),
        P(("gy", "gx"), "gz"),
        P("gz"),
    )
    out_specs = (
        P(("gy", "gx"), "gz"),
        P(("gy", "gx"), "gz"),
        P(("gz", "gy"), "gx"),
        P(("gz", "gy"), "gx"),
        P(("gx", "gy"), "gz"),
    )
    return jax.shard_map(body, mesh=mesh, in_specs=in_specs, out_specs=out_specs, check_vma=False)
```
